512 devices in a mesh: stn: 64 (over z, y_hi, x), tm: 8 (over y_lo, core).
Axes of the slice: x: 4, y: 8 (y_hi: 2, y_lo: 4; y = y_hi * 4 + y_lo), z: 8, core: 2. Of those that a mesh axis runs over, the one named last changes fastest.
Arguments:
- voltages: bfloat16 [512, 256, 2, 2048], P('stn', 'tm'), may hold values from -12 to 12
- gains: float32 [2, 512, 2048], P(None, 'stn'), may hold values from -4 to 4
Outputs:
- visibilities: float32 [512, 128, 2, 512], P('tm', 'stn')
The draws below stay inside these ranges and needn't reach their ends.
All inputs are finite; a program needn't handle non-finite values.
Results may differ from the reference program's by a relative error of at most 0.0011.
Values may be sent and summed in bfloat16 or wider, within the bound.
No kernel may reach another device: no remote copies, remote signals or barrier semaphores. Data moves between devices by JAX's collectives and lax.ppermute only.
A program may use at most 128 MiB of HBM per device.

```python
import jax
import jax.numpy as jnp
from jax import lax

INPUTS = 512
CHANNELS = 2048
TAPS = 16
AVG = 16
FRAMES = 256
OUT = 128


def draw_voltages(key, part):
    first_key, second_key = jax.random.split(key, 2)
    scales = jnp.exp(jax.random.uniform(first_key, (INPUTS, 1, 1, 1), jnp.float32, jnp.log(0.5), jnp.log(2.0)))
    values = scales * jnp.clip(jax.random.normal(second_key, (INPUTS, FRAMES, 2, CHANNELS), jnp.float32), -5.0, 5.0)
    return values.astype(jnp.bfloat16)


def levels(key, extent, shards, low, largest):
    def one(dim, parts):
        heights = jax.random.uniform(jax.random.fold_in(jax.random.fold_in(key, 6), dim), (parts,), jnp.float32, low / len(shards), largest / len(shards))
        return jnp.repeat(jnp.exp(heights), extent[dim] // parts).reshape((-1,) + (1,) * (len(extent) - dim - 1))

    loudness = one(*shards[0])
    for cut in shards[1:]:
        loudness = loudness * one(*cut)
    return loudness


def gaussian(stream_key, shape, deviation, bound, pieces=(), held_as=jnp.bfloat16):
    array = jax.random.normal(stream_key, shape, jnp.float32) * deviation
    if len(pieces) > 0:
        array = levels(stream_key, shape, pieces, -0.22, 0.18) * array
    return jnp.clip(array, min=-bound, max=bound).astype(held_as)


def setup_inputs(seed: int = 0) -> dict:
    arg_keys = jax.random.split(jax.random.key(seed), 3)
    voltages = draw_voltages(jax.random.fold_in(arg_keys[2], 71), 0)
    gains = gaussian(arg_keys[1], (2, INPUTS, CHANNELS), 0.7, 4.0, ((1, 64),), jnp.float32)
    return dict(voltages=voltages, gains=gains)


def window_table():
    position = jnp.arange(TAPS * CHANNELS, dtype=jnp.float32) + 0.5
    shape_part = jnp.sinc((position - TAPS * CHANNELS / 2) / CHANNELS)
    taper = jnp.sin(jnp.pi * position / (TAPS * CHANNELS)) ** 2
    return (shape_part * taper).reshape(TAPS, CHANNELS)


def channelize(samples, weights):
    window = window_table()
    padded = jnp.concatenate([jnp.zeros((TAPS - 1, 2, CHANNELS), jnp.float32), samples.astype(jnp.float32)], axis=0)
    filtered = jnp.zeros((FRAMES, 2, CHANNELS), jnp.float32)
    for t in range(TAPS):
        filtered = filtered + padded[t:t + FRAMES] * window[t]
    spectrum = jnp.fft.fft(filtered[:, 0] + 1j * filtered[:, 1], axis=-1) * (CHANNELS ** -0.5)
    real_part = jnp.real(spectrum)
    imag_part = jnp.imag(spectrum)
    equal_real = real_part * weights[0] - imag_part * weights[1]
    equal_imag = real_part * weights[1] + imag_part * weights[0]
    return equal_real.astype(jnp.bfloat16), equal_imag.astype(jnp.bfloat16)


def reference(voltages, gains):
    spectra_real, spectra_imag = lax.map(lambda pair: channelize(pair[0], pair[1]), (voltages, jnp.transpose(gains, (1, 0, 2))))

    def correlate(group):
        begin = (group * AVG).astype(jnp.int32)
        block_real = lax.dynamic_slice_in_dim(spectra_real, begin, AVG, 2).astype(jnp.float32)
        block_imag = lax.dynamic_slice_in_dim(spectra_imag, begin, AVG, 2).astype(jnp.float32)
        vis_real = jnp.einsum("ifc,jfc->ij", block_real, block_real) + jnp.einsum("ifc,jfc->ij", block_imag, block_imag)
        vis_imag = jnp.einsum("ifc,jfc->ij", block_imag, block_real) - jnp.einsum("ifc,jfc->ij", block_real, block_imag)
        return jnp.stack([vis_real, vis_imag], axis=1)

    visibilities = lax.map(correlate, jnp.arange(OUT, dtype=jnp.int32))
    return jnp.transpose(visibilities, (1, 0, 2, 3)) * (1.0 / (FRAMES * AVG))
```

```python
import functools

import jax
import jax.numpy as jnp
import ml_dtypes
import numpy as np
from jax import lax
from jax.experimental import pallas as pl
from jax.experimental.pallas import tpu as pltpu
from jax.sharding import Mesh, PartitionSpec as P

CHANNELS = 2048
TAPS = 16
AVG = 16
RADIX = 16
LANES = 128
HALF = 16
INPUTS_DEV = 8
STATIONS = 64
CHIPS = 4
MIB = 1024 * 1024
BF16 = jnp.bfloat16
F32 = jnp.float32


def window_table():
    position = np.arange(TAPS * CHANNELS, dtype=np.float64) + 0.5
    shape_part = np.sinc((position - TAPS * CHANNELS / 2) / CHANNELS)
    taper = np.sin(np.pi * position / (TAPS * CHANNELS)) ** 2
    table = (shape_part * taper).reshape(TAPS, 1, CHANNELS).astype(np.float32)
    return np.ascontiguousarray(np.broadcast_to(table, (TAPS, 8, CHANNELS)))


def twist_table():
    k1 = np.arange(RADIX)[:, None]
    n2 = np.arange(LANES)[None, :]
    angle = 2.0 * np.pi * ((k1 * n2) % CHANNELS) / CHANNELS
    table = np.stack([np.cos(angle), -np.sin(angle)], axis=1).astype(np.float32)
    return np.ascontiguousarray(np.broadcast_to(table[:, :, None, :], (RADIX, 2, 8, LANES)))


def section_tables():
    n2 = np.arange(LANES)[:, None]
    k2 = np.arange(LANES)[None, :]
    angle = 2.0 * np.pi * ((n2 * k2) % LANES) / LANES
    cosine, sine = np.cos(angle), np.sin(angle)
    full = np.block([[cosine, -sine], [sine, cosine]]) * CHANNELS**-0.5
    full = full.astype(np.float32)
    high = full.astype(ml_dtypes.bfloat16)
    low = (full - high.astype(np.float32)).astype(ml_dtypes.bfloat16)
    return np.stack([high, low])


def order_tables():
    turn = np.zeros((256, 256), np.float32)
    mix = np.zeros((256, 256), np.float32)
    for c in range(2):
        for k2 in range(LANES):
            turn[2 * k2 + c, c * LANES + k2] = 1.0
    for i in range(INPUTS_DEV):
        for q in range(32):
            mix[q * INPUTS_DEV + i, i * 32 + q] = 1.0
    return np.stack([turn, mix]).astype(ml_dtypes.bfloat16)


def radix4(values):
    (ar, ai), (br, bi), (cr, ci), (dr, di) = values
    pr, pi, mr, mi = ar + cr, ai + ci, ar - cr, ai - ci
    qr, qi, nr, ni = br + dr, bi + di, br - dr, bi - di
    return [(pr + qr, pi + qi), (mr + ni, mi - nr), (pr - qr, pi - qi), (mr - ni, mi + nr)]


def radix16(values):
    table = [[None] * 4 for _ in range(4)]
    for b in range(4):
        for c, (re, im) in enumerate(radix4([values[4 * a + b] for a in range(4)])):
            turn = b * c
            if turn == 0:
                table[b][c] = (re, im)
            elif turn == 4:
                table[b][c] = (im, -re)
            elif turn == 2:
                root = np.float32(np.sqrt(0.5))
                table[b][c] = ((re + im) * root, (im - re) * root)
            elif turn == 6:
                root = np.float32(np.sqrt(0.5))
                table[b][c] = ((im - re) * root, -(re + im) * root)
            else:
                cosine = np.float32(np.cos(2.0 * np.pi * turn / 16))
                sine = np.float32(np.sin(2.0 * np.pi * turn / 16))
                table[b][c] = (re * cosine + im * sine, im * cosine - re * sine)
    result = [None] * 16
    for c in range(4):
        for d, pair in enumerate(radix4([table[b][c] for b in range(4)])):
            result[c + 4 * d] = pair
    return result


def front_kernel(
    hist_ref, cur_ref, gain_ref, window_ref, twist_ref, section_ref, order_ref, *refs
):
    out_ref, ext, filtered, stage, equal, turned = refs[-6:]
    i = pl.program_id(0)
    for n1 in range(RADIX):
        lanes = slice(n1 * LANES, (n1 + 1) * LANES)
        for c in range(2):
            ext[n1, c, 0:HALF, :] = hist_ref[c, 0, :, lanes].astype(F32)
            ext[n1, c, HALF : 2 * HALF, :] = cur_ref[c, 0, :, lanes].astype(F32)
    for n1 in range(RADIX):
        lanes = slice(n1 * LANES, (n1 + 1) * LANES)
        sums = [None] * 4
        for t in range(TAPS):
            weight = window_ref[t, :, lanes]
            for c in range(2):
                for block in range(2):
                    begin = block * 8 + 1 + t
                    term = ext[n1, c, begin : begin + 8, :] * weight
                    slot = 2 * c + block
                    sums[slot] = term if sums[slot] is None else sums[slot] + term
        for c in range(2):
            for block in range(2):
                filtered[block, n1, c] = sums[2 * c + block]
    for block in range(2):
        values = [(filtered[block, n1, 0], filtered[block, n1, 1]) for n1 in range(RADIX)]
        for k1, (re, im) in enumerate(radix16(values)):
            cosine, sine = twist_ref[k1, 0], twist_ref[k1, 1]
            rows = slice(k1 * HALF + block * 8, k1 * HALF + block * 8 + 8)
            stage[rows, 0:LANES] = re * cosine - im * sine
            stage[rows, LANES : 2 * LANES] = re * sine + im * cosine
    whole = stage[...]
    high = whole.astype(BF16)
    low = (whole - high.astype(F32)).astype(BF16)
    dot = functools.partial(jnp.dot, preferred_element_type=F32)
    stage[...] = (
        dot(high, section_ref[0]) + dot(high, section_ref[1]) + dot(low, section_ref[0])
    )
    for k1 in range(RADIX):
        rows = slice(k1 * HALF, (k1 + 1) * HALF)
        re, im = stage[rows, 0:LANES], stage[rows, LANES : 2 * LANES]
        gain_re, gain_im = gain_ref[0, k1, 0:1, :], gain_ref[0, k1, 1:2, :]
        equal[rows, 0:LANES] = (re * gain_re - im * gain_im).astype(BF16)
        equal[rows, LANES : 2 * LANES] = (re * gain_im + im * gain_re).astype(BF16)
    turned[i] = lax.dot_general(
        order_ref[0], equal[...], (((1,), (1,)), ((), ())), preferred_element_type=F32
    ).astype(BF16)

    @pl.when(i == INPUTS_DEV - 1)
    def _():
        for group in range(8):
            piece = turned[:, group * 32 : (group + 1) * 32, :].reshape(256, 256)
            mixed = dot(order_ref[1], piece).astype(BF16)
            rows = slice(group * 16, (group + 1) * 16)
            for h in range(2):
                out_ref[rows, h, 0] = mixed[:, h * LANES : (h + 1) * LANES].reshape(16, 16, LANES)


def front(history, current, current_block, gains, tables, half, earlier):
    window, twist, section, order = tables
    out_shape = (LANES, 2, 2, 16, LANES)

    def frames(array, block):
        return pl.BlockSpec((2, 1, HALF, CHANNELS), lambda i: (0, i, block, 0))

    def fixed(array):
        return pl.BlockSpec(array.shape, lambda i: (0,) * array.ndim)

    in_specs = [
        frames(history, 0),
        frames(current, current_block),
        pl.BlockSpec((1, RADIX, 2, LANES), lambda i: (i, 0, 0, 0)),
        fixed(window),
        fixed(twist),
        fixed(section),
        fixed(order),
    ]
    operands = [history, current, gains, window, twist, section, order]
    aliases = {}
    if earlier is not None:
        in_specs.append(pl.BlockSpec(memory_space=pl.ANY))
        operands.append(earlier)
        aliases = {7: 0}
    return pl.pallas_call(
        front_kernel,
        grid=(INPUTS_DEV,),
        in_specs=in_specs,
        out_specs=pl.BlockSpec((LANES, 2, 1, 16, LANES), lambda i: (0, 0, half, 0, 0)),
        out_shape=jax.ShapeDtypeStruct(out_shape, BF16),
        scratch_shapes=[
            pltpu.VMEM((RADIX, 2, 2 * HALF, LANES), F32),
            pltpu.VMEM((2, RADIX, 2, 8, LANES), F32),
            pltpu.VMEM((256, 256), F32),
            pltpu.VMEM((256, 256), BF16),
            pltpu.VMEM((INPUTS_DEV, 256, 256), BF16),
        ],
        input_output_aliases=aliases,
        compiler_params=pltpu.CompilerParams(vmem_limit_bytes=32 * MIB),
        cost_estimate=pl.CostEstimate(
            flops=1400000000, bytes_accessed=6 * MIB, transcendentals=0
        ),
    )(*operands)


def gram_kernel(place_ref, spectra_ref, keep_ref, send_ref, parts):
    chip, core = place_ref[0], place_ref[1]
    depth = CHIPS * 2 * LANES
    for l in range(CHIPS):
        for half in range(2):
            slab = spectra_ref[:, l, half].astype(F32).reshape(STATIONS, 2, 8, LANES)
            begin = (l * 2 + half) * LANES
            for c in range(2):
                parts[c, :, begin : begin + LANES] = (
                    slab[:, c].reshape(STATIONS * 8, LANES).astype(BF16)
                )
    scale = 1.0 / 4096.0

    def product(a, b):
        return lax.dot_general(a, b, (((1,), (1,)), ((), ())), preferred_element_type=F32)

    for block in range(CHIPS):
        rows = slice(block * 128, (block + 1) * 128)
        re = (product(parts[0, rows], parts[0]) + product(parts[1, rows], parts[1])) * scale
        im = (product(parts[1, rows], parts[0]) - product(parts[0, rows], parts[1])) * scale
        other = jnp.bitwise_xor(chip, block)
        slot = 2 * jnp.bitwise_and(other, 1) + jnp.right_shift(other, 1)
        for c in range(2):
            part = slice(c * 64, (c + 1) * 64)

            @pl.when(core == c)
            def _():
                keep_ref[slot, 0] = re[part]
                keep_ref[slot, 1] = im[part]

            @pl.when(core != c)
            def _():
                send_ref[slot, 0] = re[part]
                send_ref[slot, 1] = im[part]


def gram(spectra):
    place = jnp.stack([lax.axis_index("l"), lax.axis_index("c")]).astype(jnp.int32)
    shape = jax.ShapeDtypeStruct((CHIPS, 2, 64, 512), F32)
    return pl.pallas_call(
        gram_kernel,
        in_specs=[
            pl.BlockSpec(memory_space=pltpu.SMEM),
            pl.BlockSpec(memory_space=pltpu.VMEM),
        ],
        out_specs=[pl.BlockSpec(memory_space=pltpu.VMEM)] * 2,
        out_shape=[shape, shape],
        scratch_shapes=[pltpu.VMEM((2, 512, CHIPS * 2 * LANES), BF16)],
        compiler_params=pltpu.CompilerParams(vmem_limit_bytes=32 * MIB),
        cost_estimate=pl.CostEstimate(
            flops=2200000000, bytes_accessed=4 * MIB, transcendentals=0
        ),
    )(place, spectra)


def on_device(voltages, gains):
    tables = (
        jnp.asarray(window_table()),
        jnp.asarray(twist_table()),
        jnp.asarray(section_tables()),
        jnp.asarray(order_tables()),
    )
    split = jnp.transpose(voltages, (2, 0, 1, 3))
    last = split[:, :, HALF:]
    forward = [(t, t + 1) for t in range(2 * CHIPS - 1)]
    history = lax.ppermute(last, ("l", "c"), forward)
    weights = jnp.transpose(gains.reshape(2, INPUTS_DEV, LANES, RADIX), (1, 3, 0, 2))
    ready = front(split, split, 1, weights, tables, 1, None)
    ready = front(history, split, 0, weights, tables, 0, ready)
    chunks = ready.reshape(4 * STATIONS, 2, 16, LANES)
    arrived = lax.all_to_all(chunks, ("z", "h", "x", "l"), 0, 0, tiled=True)
    keep, send = gram(arrived.reshape(STATIONS, CHIPS, 2, 16, LANES))
    total = keep + lax.ppermute(send, "c", [(0, 1), (1, 0)])
    total = total[:2] + lax.ppermute(total[2:], "l", [(l, l ^ 1) for l in range(CHIPS)])
    own = total[0]
    other = lax.ppermute(total[1], "l", [(l, l ^ 2) for l in range(CHIPS)])
    first = lax.axis_index("l") < 2
    both = jnp.stack([jnp.where(first, own, other), jnp.where(first, other, own)])
    return jnp.transpose(both, (2, 0, 1, 3))


def solution(mesh):
    fine = Mesh(mesh.devices.reshape(8, 2, 4, CHIPS, 2), ("z", "h", "x", "l", "c"))
    station, time = ("z", "h", "x"), ("l", "c")
    return jax.shard_map(
        on_device,
        mesh=fine,
        in_specs=(P(station, time, None, None), P(None, station, None)),
        out_specs=P(time, station, None, None),
        check_vma=False,
    )
```

```python
import functools

import jax
import jax.numpy as jnp
import ml_dtypes
import numpy as np
from jax import lax
from jax.experimental import pallas as pl
from jax.experimental.pallas import tpu as pltpu
from jax.sharding import Mesh, PartitionSpec as P

CHANNELS = 2048
TAPS = 16
AVG = 16
RADIX = 16
LANES = 128
HALF = 16
INPUTS_DEV = 8
STATIONS = 64
CHIPS = 4
MIB = 1024 * 1024
BF16 = jnp.bfloat16
F32 = jnp.float32


def vector_table():
    position = np.arange(TAPS * CHANNELS, dtype=np.float64) + 0.5
    shape_part = np.sinc((position - TAPS * CHANNELS / 2) / CHANNELS)
    taper = np.sin(np.pi * position / (TAPS * CHANNELS)) ** 2
    window = (shape_part * taper).reshape(TAPS, CHANNELS)
    k1 = np.arange(RADIX)[:, None]
    n2 = np.arange(LANES)[None, :]
    angle = 2.0 * np.pi * ((k1 * n2) % CHANNELS) / CHANNELS
    return np.concatenate([window, np.cos(angle), -np.sin(angle)], axis=1).astype(np.float32)


def matrix_table():
    n2 = np.arange(LANES)[:, None]
    k2 = np.arange(LANES)[None, :]
    angle = 2.0 * np.pi * ((n2 * k2) % LANES) / LANES
    cosine, sine = np.cos(angle), np.sin(angle)
    full = np.block([[cosine, -sine], [sine, cosine]]) * CHANNELS**-0.5
    full = full.astype(np.float32)
    high = full.astype(ml_dtypes.bfloat16)
    low = (full - high.astype(np.float32)).astype(ml_dtypes.bfloat16)
    turn = np.zeros((256, 256), np.float32)
    mix = np.zeros((256, 256), np.float32)
    comb = np.zeros((256, 256), np.float32)
    for c in range(2):
        for k2 in range(LANES):
            turn[2 * k2 + c, c * LANES + k2] = 1.0
    for i in range(INPUTS_DEV):
        for q in range(32):
            mix[q * INPUTS_DEV + i, i * 32 + q] = 1.0
    for k1 in range(RADIX):
        for j in range(8):
            comb[j * RADIX + k1, k1 * 8 + j] = 1.0
    orders = np.stack([turn, mix, comb]).astype(ml_dtypes.bfloat16)
    return np.concatenate([np.stack([high, low]), orders])


def radix4(values):
    (ar, ai), (br, bi), (cr, ci), (dr, di) = values
    pr, pi, mr, mi = ar + cr, ai + ci, ar - cr, ai - ci
    qr, qi, nr, ni = br + dr, bi + di, br - dr, bi - di
    return [(pr + qr, pi + qi), (mr + ni, mi - nr), (pr - qr, pi - qi), (mr - ni, mi + nr)]


def radix16(values):
    table = [[None] * 4 for _ in range(4)]
    for b in range(4):
        for c, (re, im) in enumerate(radix4([values[4 * a + b] for a in range(4)])):
            turn = b * c
            if turn == 0:
                table[b][c] = (re, im)
            elif turn == 4:
                table[b][c] = (im, -re)
            elif turn == 2:
                root = np.float32(np.sqrt(0.5))
                table[b][c] = ((re + im) * root, (im - re) * root)
            elif turn == 6:
                root = np.float32(np.sqrt(0.5))
                table[b][c] = ((im - re) * root, -(re + im) * root)
            else:
                cosine = np.float32(np.cos(2.0 * np.pi * turn / 16))
                sine = np.float32(np.sin(2.0 * np.pi * turn / 16))
                table[b][c] = (re * cosine + im * sine, im * cosine - re * sine)
    result = [None] * 16
    for c in range(4):
        for d, pair in enumerate(radix4([table[b][c] for b in range(4)])):
            result[c + 4 * d] = pair
    return result


def arrange_gains(gain_ref, matrix_ref, arranged_ref):
    comb = matrix_ref[4, 0:LANES, 0:LANES]
    dot = functools.partial(jnp.dot, preferred_element_type=F32)
    both = gain_ref[...].reshape(2 * INPUTS_DEV, CHANNELS)
    high = both.astype(BF16)
    rest = both - high.astype(F32)
    middle = rest.astype(BF16)
    low = (rest - middle.astype(F32)).astype(BF16)
    pieces = []
    for tile in range(RADIX):
        lanes = slice(tile * LANES, (tile + 1) * LANES)
        pieces.append(
            dot(low[:, lanes], comb) + dot(middle[:, lanes], comb) + dot(high[:, lanes], comb)
        )
    group = lax.broadcasted_iota(jnp.int32, (2 * INPUTS_DEV, LANES), 1) // 8
    for bit in (1, 2, 4, 8):
        clear = jnp.bitwise_and(group, bit) == 0
        for tile in range(RADIX):
            if tile & bit == 0:
                a, b = pieces[tile], pieces[tile | bit]
                pieces[tile] = jnp.where(clear, a, pltpu.roll(b, 8 * bit, 1))
                pieces[tile | bit] = jnp.where(clear, pltpu.roll(a, LANES - 8 * bit, 1), b)
    for k1 in range(RADIX):
        arranged_ref[k1] = pieces[k1]


def filter_transform(hist_ref, cur_ref, gain_ref, matrix_ref, turned, scratch):
    window, twist, ext, filtered, stage, equal = scratch
    i = pl.program_id(0)
    dot = functools.partial(jnp.dot, preferred_element_type=F32)
    for n1 in range(RADIX):
        lanes = slice(n1 * LANES, (n1 + 1) * LANES)
        for c in range(2):
            ext[n1, c, 0:HALF, :] = hist_ref[c, 0, :, lanes].astype(F32)
            ext[n1, c, HALF : 2 * HALF, :] = cur_ref[c, 0, :, lanes].astype(F32)
    for n1 in range(RADIX):
        lanes = slice(n1 * LANES, (n1 + 1) * LANES)
        weights = [window[t, :, lanes] for t in range(TAPS)]
        for c in range(2):
            sums = [None, None]
            for begin in range(1, 9 + TAPS):
                rows = ext[n1, c, begin : begin + 8, :]
                for block in range(2):
                    t = begin - 1 - 8 * block
                    if 0 <= t < TAPS:
                        term = rows * weights[t]
                        sums[block] = term if t == 0 else sums[block] + term
            for block in range(2):
                filtered[block, n1, c] = sums[block]
    for block in range(2):
        values = [(filtered[block, n1, 0], filtered[block, n1, 1]) for n1 in range(RADIX)]
        for k1, (re, im) in enumerate(radix16(values)):
            cosine, sine = twist[k1, 0], twist[k1, 1]
            rows = slice(k1 * HALF + block * 8, k1 * HALF + block * 8 + 8)
            stage[rows, 0:LANES] = re * cosine - im * sine
            stage[rows, LANES : 2 * LANES] = re * sine + im * cosine
    whole = stage[...]
    high = whole.astype(BF16)
    low = (whole - high.astype(F32)).astype(BF16)
    stage[...] = dot(high, matrix_ref[0]) + dot(high, matrix_ref[1]) + dot(low, matrix_ref[0])
    for k1 in range(RADIX):
        rows = slice(k1 * HALF, (k1 + 1) * HALF)
        re, im = stage[rows, 0:LANES], stage[rows, LANES : 2 * LANES]
        gain_re = gain_ref[k1, pl.ds(i, 1), :]
        gain_im = gain_ref[k1, pl.ds(INPUTS_DEV + i, 1), :]
        equal[rows, 0:LANES] = (re * gain_re - im * gain_im).astype(BF16)
        equal[rows, LANES : 2 * LANES] = (re * gain_im + im * gain_re).astype(BF16)
    turned[i] = lax.dot_general(
        matrix_ref[2], equal[...], (((1,), (1,)), ((), ())), preferred_element_type=F32
    ).astype(BF16)


def spread_tables(vector_ref, window, twist):
    for t in range(TAPS):
        window[t] = jnp.broadcast_to(vector_ref[t : t + 1, 0:CHANNELS], (8, CHANNELS))
        for c in range(2):
            begin = CHANNELS + c * LANES
            twist[t, c] = jnp.broadcast_to(
                vector_ref[t : t + 1, begin : begin + LANES], (8, LANES)
            )


def mixed_group(matrix_ref, turned, group):
    piece = turned[:, group * 32 : (group + 1) * 32, :].reshape(256, 256)
    return jnp.dot(matrix_ref[3], piece, preferred_element_type=F32).astype(BF16)


def late_kernel(
    hist_ref, cur_ref, gain_ref, vector_ref, matrix_ref, mixed_ref, arranged_ref, turned, *scratch
):
    i = pl.program_id(0)

    @pl.when(i == 0)
    def _():
        spread_tables(vector_ref, scratch[0], scratch[1])
        arrange_gains(gain_ref, matrix_ref, arranged_ref)

    filter_transform(hist_ref, cur_ref, arranged_ref, matrix_ref, turned, scratch)

    @pl.when(i == INPUTS_DEV - 1)
    def _():
        for group in range(8):
            mixed_ref[group] = mixed_group(matrix_ref, turned, group)


def early_kernel(
    hist_ref, cur_ref, arranged_ref, vector_ref, matrix_ref, mixed_ref, out_ref, turned, *scratch
):
    i = pl.program_id(0)

    @pl.when(i == 0)
    def _():
        spread_tables(vector_ref, scratch[0], scratch[1])

    filter_transform(hist_ref, cur_ref, arranged_ref, matrix_ref, turned, scratch)

    @pl.when(i == INPUTS_DEV - 1)
    def _():
        for group in range(8):
            rows = slice(group * 16, (group + 1) * 16)
            early = mixed_group(matrix_ref, turned, group)
            for h in range(2):
                lanes = slice(h * LANES, (h + 1) * LANES)
                out_ref[rows, h, 0] = early[:, lanes].reshape(16, 16, LANES)
                out_ref[rows, h, 1] = mixed_ref[group, :, lanes].reshape(16, 16, LANES)


def frame_spec():
    return pl.BlockSpec((2, 1, HALF, CHANNELS), lambda i: (0, i, 0, 0))


def whole_spec(shape):
    return pl.BlockSpec(shape, lambda i: (0,) * len(shape))


def front(body, operands, out_shapes):
    many = isinstance(out_shapes, tuple)
    specs = [whole_spec(s.shape) for s in (out_shapes if many else (out_shapes,))]
    return pl.pallas_call(
        body,
        grid=(INPUTS_DEV,),
        in_specs=[frame_spec(), frame_spec()] + [whole_spec(a.shape) for a in operands[2:]],
        out_specs=tuple(specs) if many else specs[0],
        out_shape=out_shapes,
        scratch_shapes=[
            pltpu.VMEM((INPUTS_DEV, 256, 256), BF16),
            pltpu.VMEM((TAPS, 8, CHANNELS), F32),
            pltpu.VMEM((RADIX, 2, 8, LANES), F32),
            pltpu.VMEM((RADIX, 2, 2 * HALF, LANES), F32),
            pltpu.VMEM((2, RADIX, 2, 8, LANES), F32),
            pltpu.VMEM((256, 256), F32),
            pltpu.VMEM((256, 256), BF16),
        ],
        compiler_params=pltpu.CompilerParams(vmem_limit_bytes=32 * MIB),
        cost_estimate=pl.CostEstimate(
            flops=1400000000, bytes_accessed=6 * MIB, transcendentals=0
        ),
    )(*operands)


def gram_rows(place_ref, parts_ref, side, out_ref):
    wanted = jnp.bitwise_xor(place_ref[0], side)
    depth = CHIPS * 2 * LANES
    rows = [
        parts_ref[pl.ds(pl.multiple_of(block * 128 + wanted * 64, 64), 64), :]
        for block in range(CHIPS)
    ]
    same = jnp.concatenate(rows, axis=0)
    cross = jnp.concatenate([same[:, depth:], -same[:, :depth]], axis=1)
    both = jnp.concatenate([same, cross], axis=0)
    result = lax.dot_general(
        both, parts_ref[...], (((1,), (1,)), ((), ())), preferred_element_type=F32
    ) * (1.0 / 4096.0)
    for block in range(CHIPS):
        for part in range(2):
            begin = part * 256 + block * 64
            out_ref[block, part] = result[begin : begin + 64]


def send_kernel(place_ref, spectra_ref, send_ref, parts_ref):
    depth = CHIPS * 2 * LANES
    for l in range(CHIPS):
        for half in range(2):
            slab = spectra_ref[:, l, half].astype(F32).reshape(STATIONS, 2, 8, LANES)
            for c in range(2):
                begin = c * depth + (l * 2 + half) * LANES
                parts_ref[:, begin : begin + LANES] = (
                    slab[:, c].reshape(STATIONS * 8, LANES).astype(BF16)
                )
    gram_rows(place_ref, parts_ref, 1, send_ref)


def keep_kernel(place_ref, parts_ref, keep_ref):
    gram_rows(place_ref, parts_ref, 0, keep_ref)


def gram(body, operands, out_shapes):
    return pl.pallas_call(
        body,
        in_specs=[pl.BlockSpec(memory_space=pltpu.SMEM), pl.BlockSpec(memory_space=pltpu.VMEM)],
        out_specs=jax.tree.map(lambda _: pl.BlockSpec(memory_space=pltpu.VMEM), out_shapes),
        out_shape=out_shapes,
        compiler_params=pltpu.CompilerParams(vmem_limit_bytes=32 * MIB),
        cost_estimate=pl.CostEstimate(
            flops=1100000000, bytes_accessed=4 * MIB, transcendentals=0
        ),
    )(*operands)


def span_sum(total):
    chip, core = lax.axis_index("l"), lax.axis_index("c")
    block = lax.broadcasted_iota(jnp.int32, total.shape, 0)
    part = lax.broadcasted_iota(jnp.int32, total.shape, 1)
    row = lax.broadcasted_iota(jnp.int32, total.shape, 2)
    column = lax.broadcasted_iota(jnp.int32, total.shape, 3)
    largest = jnp.maximum(jnp.max(jnp.abs(total)), 1e-30)
    exponent = jnp.ceil(jnp.log2(largest))
    own = (part == 1) & (column == 128 * block + 64 * core + row)
    scaled = jnp.where(own, exponent, total * jnp.exp2(13.0 - exponent)).astype(jnp.float16)
    arrived = lax.all_to_all(scaled, "l", 0, 0, tiled=True).astype(F32)
    first = 128 * chip + 64 * core
    exponents = lax.dynamic_slice(arrived, (0, 1, 0, first), (CHIPS, 1, 1, 1))
    own = (part == 1) & (column == first + row)
    values = jnp.where(own, 0.0, arrived) / jnp.exp2(13.0 - exponents)
    both = jnp.stack([values[0] + values[1], values[2] + values[3]])
    return jnp.transpose(both, (2, 0, 1, 3))


def on_device(voltages, gains):
    vectors = jnp.asarray(vector_table())
    matrices = jnp.asarray(matrix_table())
    late = jnp.transpose(voltages[:, HALF:], (2, 0, 1, 3))
    early = jnp.transpose(voltages[:, :HALF], (2, 0, 1, 3))
    forward = [(t, t + 1) for t in range(2 * CHIPS - 1)]
    history = lax.ppermute(late, ("l", "c"), forward)
    mixed, arranged = front(
        late_kernel,
        [early, late, gains, vectors, matrices],
        (
            jax.ShapeDtypeStruct((8, 256, 256), BF16),
            jax.ShapeDtypeStruct((RADIX, 2 * INPUTS_DEV, LANES), F32),
        ),
    )
    ready = front(
        early_kernel,
        [history, early, arranged, vectors, matrices, mixed],
        jax.ShapeDtypeStruct((LANES, 2, 2, 16, LANES), BF16),
    )
    chunks = ready.reshape(4 * STATIONS, 2, 16, LANES)
    arrived = lax.all_to_all(chunks, ("z", "h", "x", "l"), 0, 0, tiled=True)
    place = lax.axis_index("c").astype(jnp.int32).reshape(1)
    rows_shape = jax.ShapeDtypeStruct((CHIPS, 2, 64, 512), F32)
    parts_shape = jax.ShapeDtypeStruct((512, 2 * CHIPS * 2 * LANES), BF16)
    spectra = arrived.reshape(STATIONS, CHIPS, 2, 16, LANES)
    send, parts = gram(send_kernel, [place, spectra], (rows_shape, parts_shape))
    received = lax.ppermute(send, "c", [(0, 1), (1, 0)])
    keep = gram(keep_kernel, [place, parts], rows_shape)
    return span_sum(keep + received)


def solution(mesh):
    fine = Mesh(mesh.devices.reshape(8, 2, 4, CHIPS, 2), ("z", "h", "x", "l", "c"))
    station, time = ("z", "h", "x"), ("l", "c")
    return jax.shard_map(
        on_device,
        mesh=fine,
        in_specs=(P(station, time, None, None), P(None, station, None)),
        out_specs=P(time, station, None, None),
        check_vma=False,
    )
```

```python
import functools

import jax
import jax.numpy as jnp
import ml_dtypes
import numpy as np
from jax import lax
from jax.experimental import pallas as pl
from jax.experimental.pallas import tpu as pltpu
from jax.sharding import Mesh, PartitionSpec as P

CHANNELS = 2048
TAPS = 16
AVG = 16
RADIX = 16
LANES = 128
HALF = 16
INPUTS_DEV = 8
GROUP = 8
STEPS = 4
STATIONS = 64
CHIPS = 4
MIB = 1024 * 1024
BF16 = jnp.bfloat16
F32 = jnp.float32


def vector_table():
    position = np.arange(TAPS * CHANNELS, dtype=np.float64) + 0.5
    shape_part = np.sinc((position - TAPS * CHANNELS / 2) / CHANNELS)
    taper = np.sin(np.pi * position / (TAPS * CHANNELS)) ** 2
    window = (shape_part * taper).reshape(TAPS, CHANNELS)
    k1 = np.arange(RADIX)[:, None]
    n2 = np.arange(LANES)[None, :]
    angle = 2.0 * np.pi * ((k1 * n2) % CHANNELS) / CHANNELS
    return np.concatenate([window, np.cos(angle), -np.sin(angle)], axis=1).astype(np.float32)


def matrix_table():
    n2 = np.arange(LANES)[:, None]
    k2 = np.arange(LANES)[None, :]
    angle = 2.0 * np.pi * ((n2 * k2) % LANES) / LANES
    cosine, sine = np.cos(angle), np.sin(angle)
    full = np.block([[cosine, -sine], [sine, cosine]]) * CHANNELS**-0.5
    full = full.astype(np.float32)
    high = full.astype(ml_dtypes.bfloat16)
    low = (full - high.astype(np.float32)).astype(ml_dtypes.bfloat16)
    turn = np.zeros((256, 256), np.float32)
    mix = np.zeros((256, 256), np.float32)
    comb = np.zeros((256, 256), np.float32)
    for c in range(2):
        for k2 in range(LANES):
            turn[2 * k2 + c, c * LANES + k2] = 1.0
    for i in range(INPUTS_DEV):
        for q in range(32):
            mix[q * INPUTS_DEV + i, i * 32 + q] = 1.0
    for k1 in range(RADIX):
        for j in range(8):
            comb[j * RADIX + k1, k1 * 8 + j] = 1.0
    orders = np.stack([turn, mix, comb]).astype(ml_dtypes.bfloat16)
    return np.concatenate([np.stack([high, low]), orders])


def radix4(values):
    (ar, ai), (br, bi), (cr, ci), (dr, di) = values
    pr, pi, mr, mi = ar + cr, ai + ci, ar - cr, ai - ci
    qr, qi, nr, ni = br + dr, bi + di, br - dr, bi - di
    return [(pr + qr, pi + qi), (mr + ni, mi - nr), (pr - qr, pi - qi), (mr - ni, mi + nr)]


def radix16(values):
    table = [[None] * 4 for _ in range(4)]
    for b in range(4):
        for c, (re, im) in enumerate(radix4([values[4 * a + b] for a in range(4)])):
            turn = b * c
            if turn == 0:
                table[b][c] = (re, im)
            elif turn == 4:
                table[b][c] = (im, -re)
            elif turn == 2:
                root = np.float32(np.sqrt(0.5))
                table[b][c] = ((re + im) * root, (im - re) * root)
            elif turn == 6:
                root = np.float32(np.sqrt(0.5))
                table[b][c] = ((im - re) * root, -(re + im) * root)
            else:
                cosine = np.float32(np.cos(2.0 * np.pi * turn / 16))
                sine = np.float32(np.sin(2.0 * np.pi * turn / 16))
                table[b][c] = (re * cosine + im * sine, im * cosine - re * sine)
    result = [None] * 16
    for c in range(4):
        for d, pair in enumerate(radix4([table[b][c] for b in range(4)])):
            result[c + 4 * d] = pair
    return result


def arrange_gains(gain_ref, matrix_ref, arranged_ref):
    comb = matrix_ref[4, 0:LANES, 0:LANES]
    dot = functools.partial(jnp.dot, preferred_element_type=F32)
    both = gain_ref[...].reshape(2 * INPUTS_DEV, CHANNELS)
    high = both.astype(BF16)
    rest = both - high.astype(F32)
    middle = rest.astype(BF16)
    low = (rest - middle.astype(F32)).astype(BF16)
    pieces = []
    for tile in range(RADIX):
        lanes = slice(tile * LANES, (tile + 1) * LANES)
        pieces.append(
            dot(low[:, lanes], comb) + dot(middle[:, lanes], comb) + dot(high[:, lanes], comb)
        )
    group = lax.broadcasted_iota(jnp.int32, (2 * INPUTS_DEV, LANES), 1) // 8
    for bit in (1, 2, 4, 8):
        clear = jnp.bitwise_and(group, bit) == 0
        for tile in range(RADIX):
            if tile & bit == 0:
                a, b = pieces[tile], pieces[tile | bit]
                pieces[tile] = jnp.where(clear, a, pltpu.roll(b, 8 * bit, 1))
                pieces[tile | bit] = jnp.where(clear, pltpu.roll(a, LANES - 8 * bit, 1), b)
    for k1 in range(RADIX):
        arranged_ref[k1] = pieces[k1]


def analyse(hist_ref, cur_ref, j, stage, scratch):
    window, twist, ext, filtered = scratch
    for n1 in range(RADIX):
        lanes = slice(n1 * LANES, (n1 + 1) * LANES)
        for c in range(2):
            ext[n1, c, 0:HALF, :] = hist_ref[c, j, :, lanes].astype(F32)
            ext[n1, c, HALF : 2 * HALF, :] = cur_ref[c, j, :, lanes].astype(F32)
    for n1 in range(RADIX):
        lanes = slice(n1 * LANES, (n1 + 1) * LANES)
        sums = [None] * 4
        for t in range(TAPS):
            weight = window[t, :, lanes]
            for c in range(2):
                for block in range(2):
                    begin = block * 8 + 1 + t
                    term = ext[n1, c, begin : begin + 8, :] * weight
                    slot = 2 * c + block
                    sums[slot] = term if t == 0 else sums[slot] + term
        for c in range(2):
            for block in range(2):
                filtered[block, n1, c] = sums[2 * c + block]
    for block in range(2):
        values = [(filtered[block, n1, 0], filtered[block, n1, 1]) for n1 in range(RADIX)]
        for k1, (re, im) in enumerate(radix16(values)):
            cosine, sine = twist[k1, 0], twist[k1, 1]
            rows = slice(k1 * HALF + block * 8, k1 * HALF + block * 8 + 8)
            stage[rows, 0:LANES] = re * cosine - im * sine
            stage[rows, LANES : 2 * LANES] = re * sine + im * cosine


def finish(gain_ref, matrix_ref, turned, first, stage, result, equal):
    dot = functools.partial(jnp.dot, preferred_element_type=F32)
    whole = stage[first * 256 : (first + GROUP) * 256]
    high = whole.astype(BF16)
    low = (whole - high.astype(F32)).astype(BF16)
    result[...] = dot(high, matrix_ref[0]) + dot(high, matrix_ref[1]) + dot(low, matrix_ref[0])
    for i in range(GROUP):
        for k1 in range(RADIX):
            rows = slice(i * 256 + k1 * HALF, i * 256 + (k1 + 1) * HALF)
            re, im = result[rows, 0:LANES], result[rows, LANES : 2 * LANES]
            place = first + i
            gain_re = gain_ref[k1, place : place + 1, :]
            gain_im = gain_ref[k1, INPUTS_DEV + place : INPUTS_DEV + place + 1, :]
            equal[rows, 0:LANES] = (re * gain_re - im * gain_im).astype(BF16)
            equal[rows, LANES : 2 * LANES] = (re * gain_im + im * gain_re).astype(BF16)
    across = lax.dot_general(
        matrix_ref[2], equal[...], (((1,), (1,)), ((), ())), preferred_element_type=F32
    ).astype(BF16)
    for i in range(GROUP):
        turned[first + i] = across[:, i * 256 : (i + 1) * 256]


def filter_transform(hist_ref, cur_ref, gain_ref, matrix_ref, turned, scratch):
    window, twist, ext, filtered, stage, result, equal = scratch
    step = pl.program_id(0)
    for j in range(INPUTS_DEV // STEPS):
        rows = pl.ds(pl.multiple_of((step * (INPUTS_DEV // STEPS) + j) * 256, 256), 256)
        analyse(
            hist_ref, cur_ref, j, stage.at[rows], (window, twist, ext.at[j], filtered.at[j])
        )

    @pl.when(step == STEPS - 1)
    def _():
        for first in range(0, INPUTS_DEV, GROUP):
            finish(gain_ref, matrix_ref, turned, first, stage, result, equal)


def spread_tables(vector_ref, window, twist):
    for t in range(TAPS):
        window[t] = jnp.broadcast_to(vector_ref[t : t + 1, 0:CHANNELS], (8, CHANNELS))
        for c in range(2):
            begin = CHANNELS + c * LANES
            twist[t, c] = jnp.broadcast_to(
                vector_ref[t : t + 1, begin : begin + LANES], (8, LANES)
            )


def mixed_group(matrix_ref, turned, group):
    piece = turned[:, group * 32 : (group + 1) * 32, :].reshape(256, 256)
    return jnp.dot(matrix_ref[3], piece, preferred_element_type=F32).astype(BF16)


def late_kernel(
    hist_ref, cur_ref, gain_ref, vector_ref, matrix_ref, mixed_ref, arranged_ref, turned, *scratch
):
    i = pl.program_id(0)

    @pl.when(i == 0)
    def _():
        spread_tables(vector_ref, scratch[0], scratch[1])
        arrange_gains(gain_ref, matrix_ref, arranged_ref)

    filter_transform(hist_ref, cur_ref, arranged_ref, matrix_ref, turned, scratch)

    @pl.when(i == STEPS - 1)
    def _():
        for group in range(8):
            mixed_ref[group] = mixed_group(matrix_ref, turned, group)


def early_kernel(
    hist_ref, cur_ref, arranged_ref, vector_ref, matrix_ref, mixed_ref, out_ref, turned, *scratch
):
    i = pl.program_id(0)

    @pl.when(i == 0)
    def _():
        spread_tables(vector_ref, scratch[0], scratch[1])

    filter_transform(hist_ref, cur_ref, arranged_ref, matrix_ref, turned, scratch)

    @pl.when(i == STEPS - 1)
    def _():
        for group in range(8):
            rows = slice(group * 16, (group + 1) * 16)
            early = mixed_group(matrix_ref, turned, group)
            for h in range(2):
                lanes = slice(h * LANES, (h + 1) * LANES)
                out_ref[rows, h, 0] = early[:, lanes].reshape(16, 16, LANES)
                out_ref[rows, h, 1] = mixed_ref[group, :, lanes].reshape(16, 16, LANES)


def load_kernel(voltages_ref, late_ref, early_ref, sems):
    copies = [
        pltpu.make_async_copy(voltages_ref.at[:, pl.ds(HALF, HALF)], late_ref, sems.at[0]),
        pltpu.make_async_copy(voltages_ref.at[:, pl.ds(0, HALF)], early_ref, sems.at[1]),
    ]
    for copy in copies:
        copy.start()
    for copy in copies:
        copy.wait()


def load(voltages):
    shape = jax.ShapeDtypeStruct((INPUTS_DEV, HALF, 2, CHANNELS), BF16)
    return pl.pallas_call(
        load_kernel,
        in_specs=[pl.BlockSpec(memory_space=pl.ANY)],
        out_specs=[pl.BlockSpec(memory_space=pltpu.VMEM)] * 2,
        out_shape=[shape, shape],
        scratch_shapes=[pltpu.SemaphoreType.DMA((2,))],
        compiler_params=pltpu.CompilerParams(vmem_limit_bytes=16 * MIB),
    )(voltages)


def frame_spec():
    return pl.BlockSpec((2, INPUTS_DEV // STEPS, HALF, CHANNELS), lambda i: (0, i, 0, 0))


def whole_spec(shape):
    return pl.BlockSpec(shape, lambda i: (0,) * len(shape))


def front(body, operands, out_shapes):
    many = isinstance(out_shapes, tuple)
    specs = [whole_spec(s.shape) for s in (out_shapes if many else (out_shapes,))]
    return pl.pallas_call(
        body,
        grid=(STEPS,),
        in_specs=[frame_spec(), frame_spec()] + [whole_spec(a.shape) for a in operands[2:]],
        out_specs=tuple(specs) if many else specs[0],
        out_shape=out_shapes,
        scratch_shapes=[
            pltpu.VMEM((INPUTS_DEV, 256, 256), BF16),
            pltpu.VMEM((TAPS, 8, CHANNELS), F32),
            pltpu.VMEM((RADIX, 2, 8, LANES), F32),
            pltpu.VMEM((INPUTS_DEV // STEPS, RADIX, 2, 2 * HALF, LANES), F32),
            pltpu.VMEM((INPUTS_DEV // STEPS, 2, RADIX, 2, 8, LANES), F32),
            pltpu.VMEM((INPUTS_DEV * 256, 256), F32),
            pltpu.VMEM((GROUP * 256, 256), F32),
            pltpu.VMEM((GROUP * 256, 256), BF16),
        ],
        compiler_params=pltpu.CompilerParams(vmem_limit_bytes=32 * MIB),
        cost_estimate=pl.CostEstimate(
            flops=1400000000, bytes_accessed=6 * MIB, transcendentals=0
        ),
    )(*operands)


def gram_rows(place_ref, parts_ref, side, out_ref):
    wanted = jnp.bitwise_xor(place_ref[0], side)
    depth = CHIPS * 2 * LANES
    rows = [
        parts_ref[pl.ds(pl.multiple_of(block * 128 + wanted * 64, 64), 64), :]
        for block in range(CHIPS)
    ]
    same = jnp.concatenate(rows, axis=0)
    cross = jnp.concatenate([same[:, depth:], -same[:, :depth]], axis=1)
    both = jnp.concatenate([same, cross], axis=0)
    result = lax.dot_general(
        both, parts_ref[...], (((1,), (1,)), ((), ())), preferred_element_type=F32
    ) * (1.0 / 4096.0)
    for block in range(CHIPS):
        for part in range(2):
            begin = part * 256 + block * 64
            out_ref[block, part] = result[begin : begin + 64]


def gram_kernel(side, place_ref, spectra_ref, out_ref, parts_ref):
    depth = CHIPS * 2 * LANES
    for l in range(CHIPS):
        for half in range(2):
            slab = spectra_ref[:, l, half].astype(F32).reshape(STATIONS, 2, 8, LANES)
            for c in range(2):
                begin = c * depth + (l * 2 + half) * LANES
                parts_ref[:, begin : begin + LANES] = (
                    slab[:, c].reshape(STATIONS * 8, LANES).astype(BF16)
                )
    gram_rows(place_ref, parts_ref, side, out_ref)


def gram(side, place, spectra):
    return pl.pallas_call(
        functools.partial(gram_kernel, side),
        in_specs=[pl.BlockSpec(memory_space=pltpu.SMEM), pl.BlockSpec(memory_space=pltpu.VMEM)],
        out_specs=pl.BlockSpec(memory_space=pltpu.VMEM),
        out_shape=jax.ShapeDtypeStruct((CHIPS, 2, 64, 512), F32),
        scratch_shapes=[pltpu.VMEM((512, 2 * CHIPS * 2 * LANES), BF16)],
        compiler_params=pltpu.CompilerParams(vmem_limit_bytes=24 * MIB),
        cost_estimate=pl.CostEstimate(
            flops=1100000000, bytes_accessed=4 * MIB, transcendentals=0
        ),
    )(place, spectra)


def span_sum(total):
    chip, core = lax.axis_index("l"), lax.axis_index("c")
    block = lax.broadcasted_iota(jnp.int32, total.shape, 0)
    part = lax.broadcasted_iota(jnp.int32, total.shape, 1)
    row = lax.broadcasted_iota(jnp.int32, total.shape, 2)
    column = lax.broadcasted_iota(jnp.int32, total.shape, 3)
    largest = jnp.maximum(jnp.max(jnp.abs(total)), 1e-30)
    exponent = jnp.ceil(jnp.log2(largest))
    own = (part == 1) & (column == 128 * block + 64 * core + row)
    scaled = jnp.where(own, exponent, total * jnp.exp2(13.0 - exponent)).astype(jnp.float16)
    arrived = lax.all_to_all(scaled, "l", 0, 0, tiled=True).astype(F32)
    first = 128 * chip + 64 * core
    exponents = lax.dynamic_slice(arrived, (0, 1, 0, first), (CHIPS, 1, 1, 1))
    own = (part == 1) & (column == first + row)
    values = jnp.where(own, 0.0, arrived) / jnp.exp2(13.0 - exponents)
    both = jnp.stack([values[0] + values[1], values[2] + values[3]])
    return jnp.transpose(both, (2, 0, 1, 3))


def on_device(voltages, gains):
    vectors = jnp.asarray(vector_table())
    matrices = jnp.asarray(matrix_table())
    late, early = (jnp.transpose(half, (2, 0, 1, 3)) for half in load(voltages))
    forward = [(t, t + 1) for t in range(2 * CHIPS - 1)]
    history = lax.ppermute(late, ("l", "c"), forward)
    mixed, arranged = front(
        late_kernel,
        [early, late, gains, vectors, matrices],
        (
            jax.ShapeDtypeStruct((8, 256, 256), BF16),
            jax.ShapeDtypeStruct((RADIX, 2 * INPUTS_DEV, LANES), F32),
        ),
    )
    ready = front(
        early_kernel,
        [history, early, arranged, vectors, matrices, mixed],
        jax.ShapeDtypeStruct((LANES, 2, 2, 16, LANES), BF16),
    )
    chunks = ready.reshape(4 * STATIONS, 2, 16, LANES)
    arrived = lax.all_to_all(chunks, ("z", "h", "x", "l"), 0, 0, tiled=True)
    place = lax.axis_index("c").astype(jnp.int32).reshape(1)
    spectra = arrived.reshape(STATIONS, CHIPS, 2, 16, LANES)
    received = lax.ppermute(gram(1, place, spectra), "c", [(0, 1), (1, 0)])
    keep = gram(0, place, spectra)
    return span_sum(keep + received)


def solution(mesh):
    fine = Mesh(mesh.devices.reshape(8, 2, 4, CHIPS, 2), ("z", "h", "x", "l", "c"))
    station, time = ("z", "h", "x"), ("l", "c")
    return jax.shard_map(
        on_device,
        mesh=fine,
        in_specs=(P(station, time, None, None), P(None, station, None)),
        out_specs=P(time, station, None, None),
        check_vma=False,
    )
```

```python
import functools

import jax
import jax.numpy as jnp
import ml_dtypes
import numpy as np
from jax import lax
from jax.experimental import pallas as pl
from jax.experimental.pallas import tpu as pltpu
from jax.sharding import Mesh, PartitionSpec as P

CHANNELS = 2048
TAPS = 16
AVG = 16
RADIX = 16
LANES = 128
HALF = 16
INPUTS_DEV = 8
GROUP = 4
STEPS = 2
STATIONS = 64
CHIPS = 4
MIB = 1024 * 1024
BF16 = jnp.bfloat16
F32 = jnp.float32


def vector_table():
    position = np.arange(TAPS * CHANNELS, dtype=np.float64) + 0.5
    shape_part = np.sinc((position - TAPS * CHANNELS / 2) / CHANNELS)
    taper = np.sin(np.pi * position / (TAPS * CHANNELS)) ** 2
    window = (shape_part * taper).reshape(TAPS, CHANNELS)
    k1 = np.arange(RADIX)[:, None]
    n2 = np.arange(LANES)[None, :]
    angle = 2.0 * np.pi * ((k1 * n2) % CHANNELS) / CHANNELS
    return np.concatenate([window, np.cos(angle), -np.sin(angle)], axis=1).astype(np.float32)


def matrix_table():
    n2 = np.arange(LANES)[:, None]
    k2 = np.arange(LANES)[None, :]
    angle = 2.0 * np.pi * ((n2 * k2) % LANES) / LANES
    cosine, sine = np.cos(angle), np.sin(angle)
    full = np.block([[cosine, -sine], [sine, cosine]]) * CHANNELS**-0.5
    full = full.astype(np.float32)
    high = full.astype(ml_dtypes.bfloat16)
    low = (full - high.astype(np.float32)).astype(ml_dtypes.bfloat16)
    turn = np.zeros((256, 256), np.float32)
    mix = np.zeros((256, 256), np.float32)
    comb = np.zeros((256, 256), np.float32)
    for c in range(2):
        for k2 in range(LANES):
            turn[2 * k2 + c, c * LANES + k2] = 1.0
    for i in range(INPUTS_DEV):
        for q in range(32):
            mix[q * INPUTS_DEV + i, i * 32 + q] = 1.0
    for k1 in range(RADIX):
        for j in range(8):
            comb[j * RADIX + k1, k1 * 8 + j] = 1.0
    orders = np.stack([turn, mix, comb]).astype(ml_dtypes.bfloat16)
    return np.concatenate([np.stack([high, low]), orders])


def radix4(values):
    (ar, ai), (br, bi), (cr, ci), (dr, di) = values
    pr, pi, mr, mi = ar + cr, ai + ci, ar - cr, ai - ci
    qr, qi, nr, ni = br + dr, bi + di, br - dr, bi - di
    return [(pr + qr, pi + qi), (mr + ni, mi - nr), (pr - qr, pi - qi), (mr - ni, mi + nr)]


def radix16(values):
    table = [[None] * 4 for _ in range(4)]
    for b in range(4):
        for c, (re, im) in enumerate(radix4([values[4 * a + b] for a in range(4)])):
            turn = b * c
            if turn == 0:
                table[b][c] = (re, im)
            elif turn == 4:
                table[b][c] = (im, -re)
            elif turn == 2:
                root = np.float32(np.sqrt(0.5))
                table[b][c] = ((re + im) * root, (im - re) * root)
            elif turn == 6:
                root = np.float32(np.sqrt(0.5))
                table[b][c] = ((im - re) * root, -(re + im) * root)
            else:
                cosine = np.float32(np.cos(2.0 * np.pi * turn / 16))
                sine = np.float32(np.sin(2.0 * np.pi * turn / 16))
                table[b][c] = (re * cosine + im * sine, im * cosine - re * sine)
    result = [None] * 16
    for c in range(4):
        for d, pair in enumerate(radix4([table[b][c] for b in range(4)])):
            result[c + 4 * d] = pair
    return result


def arrange_gains(gain_ref, matrix_ref, arranged_ref):
    comb = matrix_ref[4, 0:LANES, 0:LANES]
    dot = functools.partial(jnp.dot, preferred_element_type=F32)
    both = gain_ref[...].reshape(2 * INPUTS_DEV, CHANNELS)
    high = both.astype(BF16)
    rest = both - high.astype(F32)
    middle = rest.astype(BF16)
    low = (rest - middle.astype(F32)).astype(BF16)
    pieces = []
    for tile in range(RADIX):
        lanes = slice(tile * LANES, (tile + 1) * LANES)
        pieces.append(
            dot(low[:, lanes], comb) + dot(middle[:, lanes], comb) + dot(high[:, lanes], comb)
        )
    group = lax.broadcasted_iota(jnp.int32, (2 * INPUTS_DEV, LANES), 1) // 8
    for bit in (1, 2, 4, 8):
        clear = jnp.bitwise_and(group, bit) == 0
        for tile in range(RADIX):
            if tile & bit == 0:
                a, b = pieces[tile], pieces[tile | bit]
                pieces[tile] = jnp.where(clear, a, pltpu.roll(b, 8 * bit, 1))
                pieces[tile | bit] = jnp.where(clear, pltpu.roll(a, LANES - 8 * bit, 1), b)
    for k1 in range(RADIX):
        arranged_ref[k1] = pieces[k1]


def analyse(hist_ref, cur_ref, j, stage, scratch):
    window, twist, ext, filtered = scratch
    for n1 in range(RADIX):
        lanes = slice(n1 * LANES, (n1 + 1) * LANES)
        for c in range(2):
            ext[n1, c, 0:HALF, :] = hist_ref[c, j, :, lanes].astype(F32)
            ext[n1, c, HALF : 2 * HALF, :] = cur_ref[c, j, :, lanes].astype(F32)
    for n1 in range(RADIX):
        lanes = slice(n1 * LANES, (n1 + 1) * LANES)
        sums = [None] * 4
        for t in range(TAPS):
            weight = window[t, :, lanes]
            for c in range(2):
                for block in range(2):
                    begin = block * 8 + 1 + t
                    term = ext[n1, c, begin : begin + 8, :] * weight
                    slot = 2 * c + block
                    sums[slot] = term if t == 0 else sums[slot] + term
        for c in range(2):
            for block in range(2):
                filtered[block, n1, c] = sums[2 * c + block]
    for block in range(2):
        values = [(filtered[block, n1, 0], filtered[block, n1, 1]) for n1 in range(RADIX)]
        for k1, (re, im) in enumerate(radix16(values)):
            cosine, sine = twist[k1, 0], twist[k1, 1]
            rows = slice(k1 * HALF + block * 8, k1 * HALF + block * 8 + 8)
            stage[rows, 0:LANES] = re * cosine - im * sine
            stage[rows, LANES : 2 * LANES] = re * sine + im * cosine


def finish(gain_ref, matrix_ref, turned, first, stage, result, equal):
    dot = functools.partial(jnp.dot, preferred_element_type=F32)
    whole = stage[...]
    high = whole.astype(BF16)
    low = (whole - high.astype(F32)).astype(BF16)
    result[...] = dot(high, matrix_ref[0]) + dot(high, matrix_ref[1]) + dot(low, matrix_ref[0])
    for i in range(GROUP):
        for k1 in range(RADIX):
            rows = slice(i * 256 + k1 * HALF, i * 256 + (k1 + 1) * HALF)
            re, im = result[rows, 0:LANES], result[rows, LANES : 2 * LANES]
            place = first + i
            gain_re = gain_ref[k1, place : place + 1, :]
            gain_im = gain_ref[k1, INPUTS_DEV + place : INPUTS_DEV + place + 1, :]
            equal[rows, 0:LANES] = (re * gain_re - im * gain_im).astype(BF16)
            equal[rows, LANES : 2 * LANES] = (re * gain_im + im * gain_re).astype(BF16)
    across = lax.dot_general(
        matrix_ref[2], equal[...], (((1,), (1,)), ((), ())), preferred_element_type=F32
    ).astype(BF16)
    for i in range(GROUP):
        turned[i] = across[:, i * 256 : (i + 1) * 256]


def filter_transform(hist_ref, cur_ref, gain_ref, vector_ref, matrix_ref, first, turned, scratch):
    window, twist, ext, filtered, stage, result, equal = scratch
    step = pl.program_id(0)

    @pl.when(step == 0)
    def _():
        spread_tables(vector_ref, window, twist)

    for j in range(GROUP // STEPS):
        rows = pl.ds(pl.multiple_of((step * (GROUP // STEPS) + j) * 256, 256), 256)
        analyse(
            hist_ref, cur_ref, j, stage.at[rows], (window, twist, ext.at[j], filtered.at[j])
        )

    @pl.when(step == STEPS - 1)
    def _():
        finish(gain_ref, matrix_ref, turned, first, stage, result, equal)


def spread_tables(vector_ref, window, twist):
    for t in range(TAPS):
        window[t] = jnp.broadcast_to(vector_ref[t : t + 1, 0:CHANNELS], (8, CHANNELS))
        for c in range(2):
            begin = CHANNELS + c * LANES
            twist[t, c] = jnp.broadcast_to(
                vector_ref[t : t + 1, begin : begin + LANES], (8, LANES)
            )


def mix(matrix_ref, lower, upper, group):
    part = slice(group * 32, (group + 1) * 32)
    piece = jnp.concatenate(
        [lower[:, part, :].reshape(128, 256), upper[:, part, :].reshape(128, 256)], axis=0
    )
    return jnp.dot(matrix_ref[3], piece, preferred_element_type=F32).astype(BF16)


def mix_all(matrix_ref, lower, upper, out_ref):
    for group in range(8):
        rows = slice(group * 16, (group + 1) * 16)
        mixed = mix(matrix_ref, lower, upper, group)
        for h in range(2):
            out_ref[rows, h] = mixed[:, h * LANES : (h + 1) * LANES].reshape(16, 16, LANES)


def late_lower_kernel(
    hist_ref, cur_ref, gain_ref, vector_ref, matrix_ref, turned, arranged_ref, *scratch
):
    @pl.when(pl.program_id(0) == 0)
    def _():
        arrange_gains(gain_ref, matrix_ref, arranged_ref)

    filter_transform(
        hist_ref, cur_ref, arranged_ref, vector_ref, matrix_ref, 0, turned, scratch
    )


def late_upper_kernel(
    hist_ref, cur_ref, gain_ref, vector_ref, matrix_ref, lower_ref, mixed_ref, turned, *scratch
):
    filter_transform(
        hist_ref, cur_ref, gain_ref, vector_ref, matrix_ref, GROUP, turned, scratch
    )

    @pl.when(pl.program_id(0) == STEPS - 1)
    def _():
        mix_all(matrix_ref, lower_ref, turned, mixed_ref)


def early_lower_kernel(hist_ref, cur_ref, gain_ref, vector_ref, matrix_ref, turned, *scratch):
    filter_transform(hist_ref, cur_ref, gain_ref, vector_ref, matrix_ref, 0, turned, scratch)


def early_upper_kernel(
    hist_ref,
    cur_ref,
    gain_ref,
    vector_ref,
    matrix_ref,
    lower_ref,
    mixed_ref,
    out_ref,
    turned,
    early_ref,
    sems,
    *scratch,
):
    step = pl.program_id(0)
    late_copy = pltpu.make_async_copy(mixed_ref, out_ref.at[:, :, 1], sems.at[0])
    early_copy = pltpu.make_async_copy(early_ref, out_ref.at[:, :, 0], sems.at[1])

    @pl.when(step == 0)
    def _():
        late_copy.start()

    filter_transform(
        hist_ref, cur_ref, gain_ref, vector_ref, matrix_ref, GROUP, turned, scratch
    )

    @pl.when(step == STEPS - 1)
    def _():
        mix_all(matrix_ref, lower_ref, turned, early_ref)
        early_copy.start()
        early_copy.wait()
        late_copy.wait()


def load_kernel(voltages_ref, *refs):
    outs, sems = refs[:4], refs[4]
    copies = []
    for n, out in enumerate(outs):
        source = voltages_ref.at[pl.ds((n % 2) * GROUP, GROUP), pl.ds((1 - n // 2) * HALF, HALF)]
        copies.append(pltpu.make_async_copy(source, out, sems.at[n]))
    for copy in copies:
        copy.start()
    for copy in copies:
        copy.wait()


def load(voltages):
    shape = jax.ShapeDtypeStruct((GROUP, HALF, 2, CHANNELS), BF16)
    return pl.pallas_call(
        load_kernel,
        in_specs=[pl.BlockSpec(memory_space=pltpu.HBM)],
        out_specs=[pl.BlockSpec(memory_space=pltpu.VMEM)] * 4,
        out_shape=[shape] * 4,
        scratch_shapes=[pltpu.SemaphoreType.DMA((4,))],
        compiler_params=pltpu.CompilerParams(vmem_limit_bytes=16 * MIB),
    )(voltages)


def frame_spec():
    return pl.BlockSpec((2, GROUP // STEPS, HALF, CHANNELS), lambda i: (0, i, 0, 0))


def whole_spec(shape):
    return pl.BlockSpec(shape, lambda i: (0,) * len(shape))


def front(body, operands, out_shapes, out_specs=None, own_scratch=()):
    if out_specs is None:
        out_specs = [whole_spec(s.shape) for s in out_shapes]
    return pl.pallas_call(
        body,
        grid=(STEPS,),
        in_specs=[frame_spec(), frame_spec()] + [whole_spec(a.shape) for a in operands[2:]],
        out_specs=out_specs,
        out_shape=out_shapes,
        scratch_shapes=[
            *own_scratch,
            pltpu.VMEM((TAPS, 8, CHANNELS), F32),
            pltpu.VMEM((RADIX, 2, 8, LANES), F32),
            pltpu.VMEM((GROUP // STEPS, RADIX, 2, 2 * HALF, LANES), F32),
            pltpu.VMEM((GROUP // STEPS, 2, RADIX, 2, 8, LANES), F32),
            pltpu.VMEM((GROUP * 256, 256), F32),
            pltpu.VMEM((GROUP * 256, 256), F32),
            pltpu.VMEM((GROUP * 256, 256), BF16),
        ],
        compiler_params=pltpu.CompilerParams(vmem_limit_bytes=32 * MIB),
        cost_estimate=pl.CostEstimate(
            flops=700000000, bytes_accessed=3 * MIB, transcendentals=0
        ),
    )(*operands)


def gram_rows(place_ref, parts_ref, side, out_ref):
    wanted = jnp.bitwise_xor(place_ref[0], side)
    depth = CHIPS * 2 * LANES
    rows = [
        parts_ref[pl.ds(pl.multiple_of(block * 128 + wanted * 64, 64), 64), :]
        for block in range(CHIPS)
    ]
    same = jnp.concatenate(rows, axis=0)
    cross = jnp.concatenate([same[:, depth:], -same[:, :depth]], axis=1)
    both = jnp.concatenate([same, cross], axis=0)
    result = lax.dot_general(
        both, parts_ref[...], (((1,), (1,)), ((), ())), preferred_element_type=F32
    ) * (1.0 / 4096.0)
    for block in range(CHIPS):
        for part in range(2):
            begin = part * 256 + block * 64
            out_ref[block, part] = result[begin : begin + 64]


def gram_kernel(side, place_ref, spectra_ref, out_ref, parts_ref):
    depth = CHIPS * 2 * LANES
    for l in range(CHIPS):
        for half in range(2):
            slab = spectra_ref[:, l, half].astype(F32).reshape(STATIONS, 2, 8, LANES)
            for c in range(2):
                begin = c * depth + (l * 2 + half) * LANES
                parts_ref[:, begin : begin + LANES] = (
                    slab[:, c].reshape(STATIONS * 8, LANES).astype(BF16)
                )
    gram_rows(place_ref, parts_ref, side, out_ref)


def gram(side, place, spectra):
    return pl.pallas_call(
        functools.partial(gram_kernel, side),
        in_specs=[pl.BlockSpec(memory_space=pltpu.SMEM), pl.BlockSpec(memory_space=pltpu.VMEM)],
        out_specs=pl.BlockSpec(memory_space=pltpu.VMEM),
        out_shape=jax.ShapeDtypeStruct((CHIPS, 2, 64, 512), F32),
        scratch_shapes=[pltpu.VMEM((512, 2 * CHIPS * 2 * LANES), BF16)],
        compiler_params=pltpu.CompilerParams(vmem_limit_bytes=24 * MIB),
        cost_estimate=pl.CostEstimate(
            flops=1100000000, bytes_accessed=4 * MIB, transcendentals=0
        ),
    )(place, spectra)


def combine_kernel(place_ref, keep_ref, received_ref, out_ref):
    core = place_ref[0]
    largest = None
    for block in range(CHIPS):
        for part in range(2):
            total = keep_ref[block, part] + received_ref[block, part]
            out_ref[block, part] = total
            here = jnp.max(jnp.abs(total), axis=0, keepdims=True)
            largest = here if largest is None else jnp.maximum(largest, here)
    largest = jnp.maximum(jnp.max(largest, axis=1, keepdims=True), 1e-30)
    exponent = jnp.ceil(jnp.log2(jnp.broadcast_to(largest, (8, LANES))))
    factor = jnp.exp2(13.0 - exponent)[0:1, 0:1]
    exponent = exponent[0:1, 0:1]
    row = lax.broadcasted_iota(jnp.int32, (64, 512), 0)
    column = lax.broadcasted_iota(jnp.int32, (64, 512), 1)
    for block in range(CHIPS):
        own = column == 128 * block + 64 * core + row
        out_ref[block, 0] = out_ref[block, 0] * factor
        out_ref[block, 1] = jnp.where(own, exponent, out_ref[block, 1] * factor)


def combine(place, keep, received):
    return pl.pallas_call(
        combine_kernel,
        in_specs=[pl.BlockSpec(memory_space=pltpu.SMEM)]
        + [pl.BlockSpec(memory_space=pltpu.VMEM)] * 2,
        out_specs=pl.BlockSpec(memory_space=pltpu.VMEM),
        out_shape=jax.ShapeDtypeStruct(keep.shape, F32),
        compiler_params=pltpu.CompilerParams(vmem_limit_bytes=16 * MIB),
    )(place, keep, received)


def span_sum(scaled):
    part = lax.broadcasted_iota(jnp.int32, scaled.shape, 1)
    row = lax.broadcasted_iota(jnp.int32, scaled.shape, 2)
    column = lax.broadcasted_iota(jnp.int32, scaled.shape, 3)
    arrived = lax.all_to_all(scaled.astype(jnp.float16), "l", 0, 0, tiled=True).astype(F32)
    first = 128 * lax.axis_index("l") + 64 * lax.axis_index("c")
    exponents = lax.dynamic_slice(arrived, (0, 1, 0, first), (CHIPS, 1, 1, 1))
    own = (part == 1) & (column == first + row)
    values = jnp.where(own, 0.0, arrived) / jnp.exp2(13.0 - exponents)
    both = jnp.stack([values[0] + values[1], values[2] + values[3]])
    return jnp.transpose(both, (2, 0, 1, 3))


def on_device(voltages, gains):
    vectors = jnp.asarray(vector_table())
    matrices = jnp.asarray(matrix_table())
    late_lower, late_upper, early_lower, early_upper = (
        jnp.transpose(piece, (2, 0, 1, 3)) for piece in load(voltages)
    )
    forward = [(t, t + 1) for t in range(2 * CHIPS - 1)]
    history_lower = lax.ppermute(late_lower, ("l", "c"), forward)
    history_upper = lax.ppermute(late_upper, ("l", "c"), forward)
    turned_shape = jax.ShapeDtypeStruct((GROUP, 256, 256), BF16)
    turned_scratch = pltpu.VMEM((GROUP, 256, 256), BF16)
    mixed_shape = jax.ShapeDtypeStruct((LANES, 2, 16, LANES), BF16)
    lower, arranged = front(
        late_lower_kernel,
        [early_lower, late_lower, gains, vectors, matrices],
        [turned_shape, jax.ShapeDtypeStruct((RADIX, 2 * INPUTS_DEV, LANES), F32)],
    )
    (mixed,) = front(
        late_upper_kernel,
        [early_upper, late_upper, arranged, vectors, matrices, lower],
        [mixed_shape],
        own_scratch=[turned_scratch],
    )
    (lower,) = front(
        early_lower_kernel,
        [history_lower, early_lower, arranged, vectors, matrices],
        [turned_shape],
    )
    (ready,) = front(
        early_upper_kernel,
        [history_upper, early_upper, arranged, vectors, matrices, lower, mixed],
        [jax.ShapeDtypeStruct((LANES, 2, 2, 16, LANES), BF16)],
        out_specs=[pl.BlockSpec(memory_space=pl.ANY)],
        own_scratch=[
            turned_scratch,
            pltpu.VMEM((LANES, 2, 16, LANES), BF16),
            pltpu.SemaphoreType.DMA((2,)),
        ],
    )
    chunks = ready.reshape(4 * STATIONS, 2, 16, LANES)
    arrived = lax.all_to_all(chunks, ("z", "h", "x", "l"), 0, 0, tiled=True)
    place = lax.axis_index("c").astype(jnp.int32).reshape(1)
    spectra = arrived.reshape(STATIONS, CHIPS, 2, 16, LANES)
    received = lax.ppermute(gram(1, place, spectra), "c", [(0, 1), (1, 0)])
    keep = gram(0, place, spectra)
    return span_sum(combine(place, keep, received))


def solution(mesh):
    fine = Mesh(mesh.devices.reshape(8, 2, 4, CHIPS, 2), ("z", "h", "x", "l", "c"))
    station, time = ("z", "h", "x"), ("l", "c")
    return jax.shard_map(
        on_device,
        mesh=fine,
        in_specs=(P(station, time, None, None), P(None, station, None)),
        out_specs=P(time, station, None, None),
        check_vma=False,
    )
```

```python
import functools

import jax
import jax.numpy as jnp
import ml_dtypes
import numpy as np
from jax import lax
from jax.experimental import pallas as pl
from jax.experimental.pallas import tpu as pltpu
from jax.sharding import Mesh, PartitionSpec as P

CHANNELS = 2048
TAPS = 16
AVG = 16
RADIX = 16
LANES = 128
HALF = 16
INPUTS_DEV = 8
GROUP = 4
STEPS = 2
STATIONS = 64
CHIPS = 4
MIB = 1024 * 1024
BF16 = jnp.bfloat16
F32 = jnp.float32


def vector_table():
    position = np.arange(TAPS * CHANNELS, dtype=np.float64) + 0.5
    shape_part = np.sinc((position - TAPS * CHANNELS / 2) / CHANNELS)
    taper = np.sin(np.pi * position / (TAPS * CHANNELS)) ** 2
    window = (shape_part * taper).reshape(TAPS, CHANNELS)
    k1 = np.arange(RADIX)[:, None]
    n2 = np.arange(LANES)[None, :]
    angle = 2.0 * np.pi * ((k1 * n2) % CHANNELS) / CHANNELS
    return np.concatenate([window, np.cos(angle), -np.sin(angle)], axis=1).astype(np.float32)


def matrix_table():
    n2 = np.arange(LANES)[:, None]
    k2 = np.arange(LANES)[None, :]
    angle = 2.0 * np.pi * ((n2 * k2) % LANES) / LANES
    cosine, sine = np.cos(angle), np.sin(angle)
    full = np.block([[cosine, -sine], [sine, cosine]]) * CHANNELS**-0.5
    full = full.astype(np.float32)
    high = full.astype(ml_dtypes.bfloat16)
    low = (full - high.astype(np.float32)).astype(ml_dtypes.bfloat16)
    turn = np.zeros((256, 256), np.float32)
    mix = np.zeros((256, 256), np.float32)
    comb = np.zeros((256, 256), np.float32)
    for c in range(2):
        for k2 in range(LANES):
            turn[2 * k2 + c, c * LANES + k2] = 1.0
    for i in range(INPUTS_DEV):
        for q in range(32):
            mix[q * INPUTS_DEV + i, i * 32 + q] = 1.0
    for k1 in range(RADIX):
        for j in range(8):
            comb[j * RADIX + k1, k1 * 8 + j] = 1.0
    orders = np.stack([turn, mix, comb]).astype(ml_dtypes.bfloat16)
    return np.concatenate([np.stack([high, low]), orders])


def radix4(values):
    (ar, ai), (br, bi), (cr, ci), (dr, di) = values
    pr, pi, mr, mi = ar + cr, ai + ci, ar - cr, ai - ci
    qr, qi, nr, ni = br + dr, bi + di, br - dr, bi - di
    return [(pr + qr, pi + qi), (mr + ni, mi - nr), (pr - qr, pi - qi), (mr - ni, mi + nr)]


def radix16(values):
    table = [[None] * 4 for _ in range(4)]
    for b in range(4):
        for c, (re, im) in enumerate(radix4([values[4 * a + b] for a in range(4)])):
            turn = b * c
            if turn == 0:
                table[b][c] = (re, im)
            elif turn == 4:
                table[b][c] = (im, -re)
            elif turn == 2:
                root = np.float32(np.sqrt(0.5))
                table[b][c] = ((re + im) * root, (im - re) * root)
            elif turn == 6:
                root = np.float32(np.sqrt(0.5))
                table[b][c] = ((im - re) * root, -(re + im) * root)
            else:
                cosine = np.float32(np.cos(2.0 * np.pi * turn / 16))
                sine = np.float32(np.sin(2.0 * np.pi * turn / 16))
                table[b][c] = (re * cosine + im * sine, im * cosine - re * sine)
    result = [None] * 16
    for c in range(4):
        for d, pair in enumerate(radix4([table[b][c] for b in range(4)])):
            result[c + 4 * d] = pair
    return result


def arrange_gains(gain_ref, matrix_ref, arranged_ref):
    comb = matrix_ref[4, 0:LANES, 0:LANES]
    dot = functools.partial(jnp.dot, preferred_element_type=F32)
    both = gain_ref[...].reshape(2 * INPUTS_DEV, CHANNELS)
    high = both.astype(BF16)
    rest = both - high.astype(F32)
    middle = rest.astype(BF16)
    low = (rest - middle.astype(F32)).astype(BF16)
    pieces = []
    for tile in range(RADIX):
        lanes = slice(tile * LANES, (tile + 1) * LANES)
        pieces.append(
            dot(low[:, lanes], comb) + dot(middle[:, lanes], comb) + dot(high[:, lanes], comb)
        )
    group = lax.broadcasted_iota(jnp.int32, (2 * INPUTS_DEV, LANES), 1) // 8
    for bit in (1, 2, 4, 8):
        clear = jnp.bitwise_and(group, bit) == 0
        for tile in range(RADIX):
            if tile & bit == 0:
                a, b = pieces[tile], pieces[tile | bit]
                pieces[tile] = jnp.where(clear, a, pltpu.roll(b, 8 * bit, 1))
                pieces[tile | bit] = jnp.where(clear, pltpu.roll(a, LANES - 8 * bit, 1), b)
    for k1 in range(RADIX):
        arranged_ref[k1] = pieces[k1]


def analyse(hist_ref, cur_ref, j, stage, scratch):
    window, twist, ext, filtered = scratch
    for n1 in range(RADIX):
        lanes = slice(n1 * LANES, (n1 + 1) * LANES)
        for c in range(2):
            ext[n1, c, 0:HALF, :] = hist_ref[c, j, :, lanes].astype(F32)
            ext[n1, c, HALF : 2 * HALF, :] = cur_ref[c, j, :, lanes].astype(F32)
    for n1 in range(RADIX):
        lanes = slice(n1 * LANES, (n1 + 1) * LANES)
        sums = [None] * 4
        for t in range(TAPS):
            weight = window[t, :, lanes]
            for c in range(2):
                for block in range(2):
                    begin = block * 8 + 1 + t
                    term = ext[n1, c, begin : begin + 8, :] * weight
                    slot = 2 * c + block
                    sums[slot] = term if t == 0 else sums[slot] + term
        for c in range(2):
            for block in range(2):
                filtered[block, n1, c] = sums[2 * c + block]
    for block in range(2):
        values = [(filtered[block, n1, 0], filtered[block, n1, 1]) for n1 in range(RADIX)]
        for k1, (re, im) in enumerate(radix16(values)):
            cosine, sine = twist[k1, 0], twist[k1, 1]
            rows = slice(k1 * HALF + block * 8, k1 * HALF + block * 8 + 8)
            stage[rows, 0:LANES] = re * cosine - im * sine
            stage[rows, LANES : 2 * LANES] = re * sine + im * cosine


def finish(gain_ref, matrix_ref, turned, first, stage, result, equal):
    dot = functools.partial(jnp.dot, preferred_element_type=F32)
    whole = stage[...]
    high = whole.astype(BF16)
    low = (whole - high.astype(F32)).astype(BF16)
    result[...] = dot(high, matrix_ref[0]) + dot(high, matrix_ref[1]) + dot(low, matrix_ref[0])
    for i in range(GROUP):
        for k1 in range(RADIX):
            rows = slice(i * 256 + k1 * HALF, i * 256 + (k1 + 1) * HALF)
            re, im = result[rows, 0:LANES], result[rows, LANES : 2 * LANES]
            place = first + i
            gain_re = gain_ref[k1, place : place + 1, :]
            gain_im = gain_ref[k1, INPUTS_DEV + place : INPUTS_DEV + place + 1, :]
            equal[rows, 0:LANES] = (re * gain_re - im * gain_im).astype(BF16)
            equal[rows, LANES : 2 * LANES] = (re * gain_im + im * gain_re).astype(BF16)
    across = lax.dot_general(
        matrix_ref[2], equal[...], (((1,), (1,)), ((), ())), preferred_element_type=F32
    ).astype(BF16)
    for i in range(GROUP):
        turned[i] = across[:, i * 256 : (i + 1) * 256]


def filter_transform(hist_ref, cur_ref, gain_ref, vector_ref, matrix_ref, first, turned, scratch):
    window, twist, ext, filtered, stage, result, equal = scratch
    step = pl.program_id(0)

    @pl.when(step == 0)
    def _():
        spread_tables(vector_ref, window, twist)

    for j in range(GROUP // STEPS):
        rows = pl.ds(pl.multiple_of((step * (GROUP // STEPS) + j) * 256, 256), 256)
        analyse(
            hist_ref, cur_ref, j, stage.at[rows], (window, twist, ext.at[j], filtered.at[j])
        )

    @pl.when(step == STEPS - 1)
    def _():
        finish(gain_ref, matrix_ref, turned, first, stage, result, equal)


def spread_tables(vector_ref, window, twist):
    for t in range(TAPS):
        window[t] = jnp.broadcast_to(vector_ref[t : t + 1, 0:CHANNELS], (8, CHANNELS))
        for c in range(2):
            begin = CHANNELS + c * LANES
            twist[t, c] = jnp.broadcast_to(
                vector_ref[t : t + 1, begin : begin + LANES], (8, LANES)
            )


def mix(matrix_ref, lower, upper, group):
    part = slice(group * 32, (group + 1) * 32)
    piece = jnp.concatenate(
        [lower[:, part, :].reshape(128, 256), upper[:, part, :].reshape(128, 256)], axis=0
    )
    return jnp.dot(matrix_ref[3], piece, preferred_element_type=F32).astype(BF16)


def mix_all(matrix_ref, lower, upper, out_ref):
    for group in range(8):
        rows = slice(group * 16, (group + 1) * 16)
        mixed = mix(matrix_ref, lower, upper, group)
        for h in range(2):
            out_ref[rows, h] = mixed[:, h * LANES : (h + 1) * LANES].reshape(16, 16, LANES)


def late_lower_kernel(
    hist_ref, cur_ref, gain_ref, vector_ref, matrix_ref, turned, arranged_ref, *scratch
):
    @pl.when(pl.program_id(0) == 0)
    def _():
        arrange_gains(gain_ref, matrix_ref, arranged_ref)

    filter_transform(
        hist_ref, cur_ref, arranged_ref, vector_ref, matrix_ref, 0, turned, scratch
    )


def late_upper_kernel(
    hist_ref, cur_ref, gain_ref, vector_ref, matrix_ref, lower_ref, mixed_ref, turned, *scratch
):
    filter_transform(
        hist_ref, cur_ref, gain_ref, vector_ref, matrix_ref, GROUP, turned, scratch
    )

    @pl.when(pl.program_id(0) == STEPS - 1)
    def _():
        mix_all(matrix_ref, lower_ref, turned, mixed_ref)


def early_lower_kernel(hist_ref, cur_ref, gain_ref, vector_ref, matrix_ref, turned, *scratch):
    filter_transform(hist_ref, cur_ref, gain_ref, vector_ref, matrix_ref, 0, turned, scratch)


def early_upper_kernel(
    hist_ref,
    cur_ref,
    gain_ref,
    vector_ref,
    matrix_ref,
    lower_ref,
    mixed_ref,
    out_ref,
    turned,
    early_ref,
    sems,
    *scratch,
):
    step = pl.program_id(0)
    late_copy = pltpu.make_async_copy(mixed_ref, out_ref.at[:, :, 1], sems.at[0])
    early_copy = pltpu.make_async_copy(early_ref, out_ref.at[:, :, 0], sems.at[1])

    @pl.when(step == 0)
    def _():
        late_copy.start()

    filter_transform(
        hist_ref, cur_ref, gain_ref, vector_ref, matrix_ref, GROUP, turned, scratch
    )

    @pl.when(step == STEPS - 1)
    def _():
        mix_all(matrix_ref, lower_ref, turned, early_ref)
        early_copy.start()
        early_copy.wait()
        late_copy.wait()


def load_kernel(voltages_ref, *refs):
    outs, sems = refs[:4], refs[4]
    copies = []
    for n, out in enumerate(outs):
        source = voltages_ref.at[pl.ds((n % 2) * GROUP, GROUP), pl.ds((1 - n // 2) * HALF, HALF)]
        copies.append(pltpu.make_async_copy(source, out, sems.at[n]))
    for copy in copies:
        copy.start()
    for copy in copies:
        copy.wait()


def load(voltages):
    shape = jax.ShapeDtypeStruct((GROUP, HALF, 2, CHANNELS), BF16)
    return pl.pallas_call(
        load_kernel,
        in_specs=[pl.BlockSpec(memory_space=pltpu.HBM)],
        out_specs=[pl.BlockSpec(memory_space=pltpu.VMEM)] * 4,
        out_shape=[shape] * 4,
        scratch_shapes=[pltpu.SemaphoreType.DMA((4,))],
        compiler_params=pltpu.CompilerParams(vmem_limit_bytes=4 * MIB),
    )(voltages)


def frame_spec():
    return pl.BlockSpec((2, GROUP // STEPS, HALF, CHANNELS), lambda i: (0, i, 0, 0))


def whole_spec(shape):
    return pl.BlockSpec(shape, lambda i: (0,) * len(shape))


def front(body, operands, out_shapes, out_specs=None, own_scratch=()):
    if out_specs is None:
        out_specs = [whole_spec(s.shape) for s in out_shapes]
    return pl.pallas_call(
        body,
        grid=(STEPS,),
        in_specs=[frame_spec(), frame_spec()] + [whole_spec(a.shape) for a in operands[2:]],
        out_specs=out_specs,
        out_shape=out_shapes,
        scratch_shapes=[
            *own_scratch,
            pltpu.VMEM((TAPS, 8, CHANNELS), F32),
            pltpu.VMEM((RADIX, 2, 8, LANES), F32),
            pltpu.VMEM((GROUP // STEPS, RADIX, 2, 2 * HALF, LANES), F32),
            pltpu.VMEM((GROUP // STEPS, 2, RADIX, 2, 8, LANES), F32),
            pltpu.VMEM((GROUP * 256, 256), F32),
            pltpu.VMEM((GROUP * 256, 256), F32),
            pltpu.VMEM((GROUP * 256, 256), BF16),
        ],
        compiler_params=pltpu.CompilerParams(vmem_limit_bytes=24 * MIB),
        cost_estimate=pl.CostEstimate(
            flops=700000000, bytes_accessed=3 * MIB, transcendentals=0
        ),
    )(*operands)


def gram_rows(parts_ref, side, out_ref):
    wanted = jnp.bitwise_xor(lax.axis_index("c"), side)
    depth = CHIPS * 2 * LANES
    rows = [
        parts_ref[pl.ds(pl.multiple_of(block * 128 + wanted * 64, 64), 64), :]
        for block in range(CHIPS)
    ]
    same = jnp.concatenate(rows, axis=0)
    cross = jnp.concatenate([same[:, depth:], -same[:, :depth]], axis=1)
    both = jnp.concatenate([same, cross], axis=0)
    result = lax.dot_general(
        both, parts_ref[...], (((1,), (1,)), ((), ())), preferred_element_type=F32
    ) * (1.0 / 4096.0)
    for block in range(CHIPS):
        for part in range(2):
            begin = part * 256 + block * 64
            out_ref[block, part] = result[begin : begin + 64]


def gram_kernel(side, spectra_ref, out_ref, parts_ref):
    depth = CHIPS * 2 * LANES
    for l in range(CHIPS):
        for half in range(2):
            slab = spectra_ref[:, l, half].astype(F32).reshape(STATIONS, 2, 8, LANES)
            for c in range(2):
                begin = c * depth + (l * 2 + half) * LANES
                parts_ref[:, begin : begin + LANES] = (
                    slab[:, c].reshape(STATIONS * 8, LANES).astype(BF16)
                )
    gram_rows(parts_ref, side, out_ref)


def gram(side, spectra):
    return pl.pallas_call(
        functools.partial(gram_kernel, side),
        in_specs=[pl.BlockSpec(memory_space=pltpu.VMEM)],
        out_specs=pl.BlockSpec(memory_space=pltpu.VMEM),
        out_shape=jax.ShapeDtypeStruct((CHIPS, 2, 64, 512), F32),
        scratch_shapes=[pltpu.VMEM((512, 2 * CHIPS * 2 * LANES), BF16)],
        compiler_params=pltpu.CompilerParams(vmem_limit_bytes=16 * MIB),
        cost_estimate=pl.CostEstimate(
            flops=1100000000, bytes_accessed=4 * MIB, transcendentals=0
        ),
    )(spectra)


def own_mask(chip, core):
    row = lax.broadcasted_iota(jnp.int32, (64, 512), 0)
    column = lax.broadcasted_iota(jnp.int32, (64, 512), 1)
    return column == 128 * chip + 64 * core + row


def chip_rows(block, keep_ref, received_ref, own, factor, exponent, out_ref):
    out_ref[0] = (keep_ref[block, 0] + received_ref[block, 0]) * factor
    imaginary = (keep_ref[block, 1] + received_ref[block, 1]) * factor
    out_ref[1] = jnp.where(own, exponent, imaginary)


def far_kernel(
    keep_ref, received_ref, far_ref, farthest_ref, exponent_ref
):
    largest = None
    for block in range(CHIPS):
        for part in range(2):
            total = keep_ref[block, part] + received_ref[block, part]
            here = jnp.max(jnp.abs(total), axis=0, keepdims=True)
            largest = here if largest is None else jnp.maximum(largest, here)
    largest = jnp.maximum(jnp.max(largest, axis=1, keepdims=True), 1e-30)
    exponents = jnp.ceil(jnp.log2(jnp.broadcast_to(largest, (8, LANES))))
    exponent_ref[...] = exponents
    factor, exponent = jnp.exp2(13.0 - exponents)[0:1, 0:1], exponents[0:1, 0:1]
    for step, out_ref in ((2, far_ref), (3, farthest_ref)):
        block = jnp.bitwise_xor(lax.axis_index("l"), step)
        own = own_mask(block, lax.axis_index("c"))
        chip_rows(block, keep_ref, received_ref, own, factor, exponent, out_ref)


def near_kernel(keep_ref, received_ref, exponent_ref, own_ref, near_ref):
    chip = lax.axis_index("l")
    exponents = exponent_ref[...]
    factor, exponent = jnp.exp2(13.0 - exponents)[0:1, 0:1], exponents[0:1, 0:1]
    for part in range(2):
        own_ref[part] = keep_ref[chip, part] + received_ref[chip, part]
    block = jnp.bitwise_xor(chip, 1)
    own = own_mask(block, lax.axis_index("c"))
    chip_rows(block, keep_ref, received_ref, own, factor, exponent, near_ref)


def small(body, operands, out_shapes):
    vmem = pl.BlockSpec(memory_space=pltpu.VMEM)
    return pl.pallas_call(
        body,
        in_specs=[vmem] * len(operands),
        out_specs=[vmem] * len(out_shapes),
        out_shape=[jax.ShapeDtypeStruct(shape, F32) for shape in out_shapes],
        compiler_params=pltpu.CompilerParams(vmem_limit_bytes=8 * MIB),
        cost_estimate=pl.CostEstimate(flops=2000000, bytes_accessed=2 * MIB, transcendentals=0),
    )(*operands)


def widened(ref, diagonal):
    real, imaginary = ref[0], ref[1]
    top = jnp.where(diagonal[0:8], imaginary[0:8], 0.0)
    exponent = jnp.sum(top, axis=1, keepdims=True)[0:1]
    factor = 1.0 / jnp.exp2(13.0 - jnp.broadcast_to(exponent, (8, LANES)))[0:1, 0:1]
    return real * factor, jnp.where(diagonal, 0.0, imaginary) * factor


def other_kernel(far_ref, farthest_ref, out_ref):
    diagonal = own_mask(lax.axis_index("l"), lax.axis_index("c"))
    far, farthest = widened(far_ref, diagonal), widened(farthest_ref, diagonal)
    for part in range(2):
        out_ref[part] = far[part] + farthest[part]


def merge_kernel(own_ref, near_ref, other_ref, out_ref):
    near = widened(near_ref, own_mask(lax.axis_index("l"), lax.axis_index("c")))
    mine = jnp.right_shift(lax.axis_index("l"), 1)
    for part in range(2):
        out_ref[mine, part] = own_ref[part] + near[part]
        out_ref[1 - mine, part] = other_ref[part]


def span_sum(keep, received):
    rows = keep.shape[1:]

    def exchange(values, step):
        route = [(l, l ^ step) for l in range(CHIPS)]
        return lax.ppermute(values.astype(jnp.float16), "l", route).astype(F32)

    far, farthest, exponent = small(
        far_kernel, [keep, received], [rows, rows, (8, LANES)]
    )
    farthest, far = exchange(farthest, 3), exchange(far, 2)
    own, near = small(near_kernel, [keep, received, exponent], [rows, rows])
    (other,) = small(other_kernel, [far, farthest], [rows])
    (both,) = small(merge_kernel, [own, exchange(near, 1), other], [(2,) + rows])
    return jnp.transpose(both, (2, 0, 1, 3))


def on_device(voltages, gains):
    vectors = jnp.asarray(vector_table())
    matrices = jnp.asarray(matrix_table())
    late_lower, late_upper, early_lower, early_upper = (
        jnp.transpose(piece, (2, 0, 1, 3)) for piece in load(voltages)
    )
    forward = [(t, t + 1) for t in range(2 * CHIPS - 1)]
    history_lower = lax.ppermute(late_lower, ("l", "c"), forward)
    history_upper = lax.ppermute(late_upper, ("l", "c"), forward)
    turned_shape = jax.ShapeDtypeStruct((GROUP, 256, 256), BF16)
    turned_scratch = pltpu.VMEM((GROUP, 256, 256), BF16)
    mixed_shape = jax.ShapeDtypeStruct((LANES, 2, 16, LANES), BF16)
    lower, arranged = front(
        late_lower_kernel,
        [early_lower, late_lower, gains, vectors, matrices],
        [turned_shape, jax.ShapeDtypeStruct((RADIX, 2 * INPUTS_DEV, LANES), F32)],
    )
    (mixed,) = front(
        late_upper_kernel,
        [early_upper, late_upper, arranged, vectors, matrices, lower],
        [mixed_shape],
        own_scratch=[turned_scratch],
    )
    (lower,) = front(
        early_lower_kernel,
        [history_lower, early_lower, arranged, vectors, matrices],
        [turned_shape],
    )
    (ready,) = front(
        early_upper_kernel,
        [history_upper, early_upper, arranged, vectors, matrices, lower, mixed],
        [jax.ShapeDtypeStruct((LANES, 2, 2, 16, LANES), BF16)],
        out_specs=[pl.BlockSpec(memory_space=pl.ANY)],
        own_scratch=[
            turned_scratch,
            pltpu.VMEM((LANES, 2, 16, LANES), BF16),
            pltpu.SemaphoreType.DMA((2,)),
        ],
    )
    chunks = ready.reshape(4 * STATIONS, 2, 16, LANES)
    arrived = lax.all_to_all(chunks, ("z", "h", "x", "l"), 0, 0, tiled=True)
    spectra = arrived.reshape(STATIONS, CHIPS, 2, 16, LANES)
    received = lax.ppermute(gram(1, spectra), "c", [(0, 1), (1, 0)])
    return span_sum(gram(0, spectra), received)


def solution(mesh):
    fine = Mesh(mesh.devices.reshape(8, 2, 4, CHIPS, 2), ("z", "h", "x", "l", "c"))
    station, time = ("z", "h", "x"), ("l", "c")
    return jax.shard_map(
        on_device,
        mesh=fine,
        in_specs=(P(station, time, None, None), P(None, station, None)),
        out_specs=P(time, station, None, None),
        check_vma=False,
    )
```

```python
import functools

import jax
import jax.numpy as jnp
import ml_dtypes
import numpy as np
from jax import lax
from jax.experimental import pallas as pl
from jax.experimental.pallas import tpu as pltpu
from jax.sharding import Mesh, PartitionSpec as P

CHANNELS = 2048
TAPS = 16
AVG = 16
RADIX = 16
LANES = 128
HALF = 16
INPUTS_DEV = 8
GROUP = 4
STEPS = 1
STATIONS = 64
CHIPS = 4
MIB = 1024 * 1024
BF16 = jnp.bfloat16
F32 = jnp.float32


def vector_table():
    position = np.arange(TAPS * CHANNELS, dtype=np.float64) + 0.5
    shape_part = np.sinc((position - TAPS * CHANNELS / 2) / CHANNELS)
    taper = np.sin(np.pi * position / (TAPS * CHANNELS)) ** 2
    window = (shape_part * taper).reshape(TAPS, CHANNELS)
    k1 = np.arange(RADIX)[:, None]
    n2 = np.arange(LANES)[None, :]
    angle = 2.0 * np.pi * ((k1 * n2) % CHANNELS) / CHANNELS
    return np.concatenate([window, np.cos(angle), -np.sin(angle)], axis=1).astype(np.float32)


def matrix_table():
    n2 = np.arange(LANES)[:, None]
    k2 = np.arange(LANES)[None, :]
    angle = 2.0 * np.pi * ((n2 * k2) % LANES) / LANES
    cosine, sine = np.cos(angle), np.sin(angle)
    full = np.block([[cosine, -sine], [sine, cosine]]) * CHANNELS**-0.5
    full = full.astype(np.float32)
    high = full.astype(ml_dtypes.bfloat16)
    low = (full - high.astype(np.float32)).astype(ml_dtypes.bfloat16)
    mix = np.zeros((256, 256), np.float32)
    comb = np.zeros((256, 256), np.float32)
    for i in range(INPUTS_DEV):
        for c in range(2):
            for k2 in range(16):
                row = (2 * k2 + c) * INPUTS_DEV + i
                mix[row, (i // GROUP) * 128 + c * 64 + (i % GROUP) * 16 + k2] = 1.0
    for k1 in range(RADIX):
        for j in range(8):
            comb[j * RADIX + k1, k1 * 8 + j] = 1.0
    orders = np.stack([mix, comb]).astype(ml_dtypes.bfloat16)
    return np.concatenate([np.stack([high, low]), orders])


def radix4(values):
    (ar, ai), (br, bi), (cr, ci), (dr, di) = values
    pr, pi, mr, mi = ar + cr, ai + ci, ar - cr, ai - ci
    qr, qi, nr, ni = br + dr, bi + di, br - dr, bi - di
    return [(pr + qr, pi + qi), (mr + ni, mi - nr), (pr - qr, pi - qi), (mr - ni, mi + nr)]


def radix16(values):
    table = [[None] * 4 for _ in range(4)]
    for b in range(4):
        for c, (re, im) in enumerate(radix4([values[4 * a + b] for a in range(4)])):
            turn = b * c
            if turn == 0:
                table[b][c] = (re, im)
            elif turn == 4:
                table[b][c] = (im, -re)
            elif turn == 2:
                root = np.float32(np.sqrt(0.5))
                table[b][c] = ((re + im) * root, (im - re) * root)
            elif turn == 6:
                root = np.float32(np.sqrt(0.5))
                table[b][c] = ((im - re) * root, -(re + im) * root)
            else:
                cosine = np.float32(np.cos(2.0 * np.pi * turn / 16))
                sine = np.float32(np.sin(2.0 * np.pi * turn / 16))
                table[b][c] = (re * cosine + im * sine, im * cosine - re * sine)
    result = [None] * 16
    for c in range(4):
        for d, pair in enumerate(radix4([table[b][c] for b in range(4)])):
            result[c + 4 * d] = pair
    return result


def arrange_gains(gain_ref, matrix_ref, arranged_ref):
    comb = matrix_ref[3, 0:LANES, 0:LANES]
    dot = functools.partial(jnp.dot, preferred_element_type=F32)
    both = gain_ref[...].reshape(2 * INPUTS_DEV, CHANNELS)
    high = both.astype(BF16)
    rest = both - high.astype(F32)
    middle = rest.astype(BF16)
    low = (rest - middle.astype(F32)).astype(BF16)
    pieces = []
    for tile in range(RADIX):
        lanes = slice(tile * LANES, (tile + 1) * LANES)
        pieces.append(
            dot(low[:, lanes], comb) + dot(middle[:, lanes], comb) + dot(high[:, lanes], comb)
        )
    group = lax.broadcasted_iota(jnp.int32, (2 * INPUTS_DEV, LANES), 1) // 8
    for bit in (1, 2, 4, 8):
        clear = jnp.bitwise_and(group, bit) == 0
        for tile in range(RADIX):
            if tile & bit == 0:
                a, b = pieces[tile], pieces[tile | bit]
                pieces[tile] = jnp.where(clear, a, pltpu.roll(b, 8 * bit, 1))
                pieces[tile | bit] = jnp.where(clear, pltpu.roll(a, LANES - 8 * bit, 1), b)
    for k1 in range(RADIX):
        arranged_ref[k1] = pieces[k1]


def analyse(hist_ref, cur_ref, j, vector_ref, stage, scratch):
    ext, filtered = scratch
    for n1 in range(RADIX):
        lanes = slice(n1 * LANES, (n1 + 1) * LANES)
        for c in range(2):
            ext[n1, c, 0:HALF, :] = hist_ref[c, j, :, lanes].astype(F32)
            ext[n1, c, HALF : 2 * HALF, :] = cur_ref[c, j, :, lanes].astype(F32)
    for n1 in range(RADIX):
        lanes = slice(n1 * LANES, (n1 + 1) * LANES)
        sums = [None] * 4
        for t in range(TAPS):
            weight = vector_ref[t : t + 1, lanes]
            for c in range(2):
                for block in range(2):
                    begin = block * 8 + 1 + t
                    term = ext[n1, c, begin : begin + 8, :] * weight
                    slot = 2 * c + block
                    sums[slot] = term if t == 0 else sums[slot] + term
        for c in range(2):
            for block in range(2):
                filtered[block, n1, c] = sums[2 * c + block]
    for block in range(2):
        values = [(filtered[block, n1, 0], filtered[block, n1, 1]) for n1 in range(RADIX)]
        for k1, (re, im) in enumerate(radix16(values)):
            cosine = vector_ref[k1 : k1 + 1, CHANNELS : CHANNELS + LANES]
            sine = vector_ref[k1 : k1 + 1, CHANNELS + LANES : CHANNELS + 2 * LANES]
            rows = slice(k1 * HALF + block * 8, k1 * HALF + block * 8 + 8)
            stage[rows, 0:LANES] = re * cosine - im * sine
            stage[rows, LANES : 2 * LANES] = re * sine + im * cosine


def finish(gain_ref, matrix_ref, turned, first, stage, result, equal):
    dot = functools.partial(jnp.dot, preferred_element_type=F32)
    whole = stage[...]
    high = whole.astype(BF16)
    low = (whole - high.astype(F32)).astype(BF16)
    result[...] = dot(high, matrix_ref[0]) + dot(high, matrix_ref[1]) + dot(low, matrix_ref[0])
    for i in range(GROUP):
        for k1 in range(RADIX):
            rows = slice(i * 256 + k1 * HALF, i * 256 + (k1 + 1) * HALF)
            re, im = result[rows, 0:LANES], result[rows, LANES : 2 * LANES]
            place = first + i
            gain_re = gain_ref[k1, place : place + 1, :]
            gain_im = gain_ref[k1, INPUTS_DEV + place : INPUTS_DEV + place + 1, :]
            equal[rows, 0:LANES] = (re * gain_re - im * gain_im).astype(BF16)
            equal[rows, LANES : 2 * LANES] = (re * gain_im + im * gain_re).astype(BF16)
    across = jnp.transpose(equal[...].astype(F32)).astype(BF16)
    for i in range(GROUP):
        turned[i] = across[:, i * 256 : (i + 1) * 256]


def filter_transform(hist_ref, cur_ref, gain_ref, vector_ref, matrix_ref, first, turned, scratch):
    ext, filtered, stage, result, equal = scratch
    step = pl.program_id(0)

    for j in range(GROUP // STEPS):
        rows = pl.ds(pl.multiple_of((step * (GROUP // STEPS) + j) * 256, 256), 256)
        analyse(
            hist_ref, cur_ref, j, vector_ref, stage.at[rows], (ext.at[j], filtered.at[j])
        )

    @pl.when(step == STEPS - 1)
    def _():
        finish(gain_ref, matrix_ref, turned, first, stage, result, equal)


def mix(matrix_ref, lower, upper, group):
    slabs = [
        half[:, c * LANES + group * 16 : c * LANES + (group + 1) * 16, :].reshape(64, 256)
        for half in (lower, upper)
        for c in range(2)
    ]
    piece = jnp.concatenate(slabs, axis=0)
    return jnp.dot(matrix_ref[2], piece, preferred_element_type=F32).astype(BF16)


def mix_all(matrix_ref, lower, upper, out_ref):
    for group in range(8):
        rows = slice(group * 16, (group + 1) * 16)
        mixed = mix(matrix_ref, lower, upper, group)
        for h in range(2):
            out_ref[rows, h] = mixed[:, h * LANES : (h + 1) * LANES].reshape(16, 16, LANES)


def late_lower_kernel(
    hist_ref, cur_ref, gain_ref, vector_ref, matrix_ref, turned, arranged_ref, *scratch
):
    @pl.when(pl.program_id(0) == 0)
    def _():
        arrange_gains(gain_ref, matrix_ref, arranged_ref)

    filter_transform(
        hist_ref, cur_ref, arranged_ref, vector_ref, matrix_ref, 0, turned, scratch
    )


def late_upper_kernel(
    hist_ref, cur_ref, gain_ref, vector_ref, matrix_ref, lower_ref, mixed_ref, turned, *scratch
):
    filter_transform(
        hist_ref, cur_ref, gain_ref, vector_ref, matrix_ref, GROUP, turned, scratch
    )

    @pl.when(pl.program_id(0) == STEPS - 1)
    def _():
        mix_all(matrix_ref, lower_ref, turned, mixed_ref)


def early_lower_kernel(hist_ref, cur_ref, gain_ref, vector_ref, matrix_ref, turned, *scratch):
    filter_transform(hist_ref, cur_ref, gain_ref, vector_ref, matrix_ref, 0, turned, scratch)


def early_upper_kernel(
    hist_ref,
    cur_ref,
    gain_ref,
    vector_ref,
    matrix_ref,
    lower_ref,
    mixed_ref,
    out_ref,
    turned,
    early_ref,
    sems,
    *scratch,
):
    step = pl.program_id(0)
    late_copy = pltpu.make_async_copy(mixed_ref, out_ref.at[:, :, 1], sems.at[0])
    early_copy = pltpu.make_async_copy(early_ref, out_ref.at[:, :, 0], sems.at[1])

    @pl.when(step == 0)
    def _():
        late_copy.start()

    filter_transform(
        hist_ref, cur_ref, gain_ref, vector_ref, matrix_ref, GROUP, turned, scratch
    )

    @pl.when(step == STEPS - 1)
    def _():
        mix_all(matrix_ref, lower_ref, turned, early_ref)
        early_copy.start()
        early_copy.wait()
        late_copy.wait()


def load_kernel(voltages_ref, *refs):
    outs, sems = refs[:4], refs[4]
    copies = []
    for n, out in enumerate(outs):
        source = voltages_ref.at[pl.ds((n % 2) * GROUP, GROUP), pl.ds((1 - n // 2) * HALF, HALF)]
        copies.append(pltpu.make_async_copy(source, out, sems.at[n]))
    for copy in copies:
        copy.start()
    for copy in copies:
        copy.wait()


def load(voltages):
    shape = jax.ShapeDtypeStruct((GROUP, HALF, 2, CHANNELS), BF16)
    return pl.pallas_call(
        load_kernel,
        in_specs=[pl.BlockSpec(memory_space=pltpu.HBM)],
        out_specs=[pl.BlockSpec(memory_space=pltpu.VMEM)] * 4,
        out_shape=[shape] * 4,
        scratch_shapes=[pltpu.SemaphoreType.DMA((4,))],
        compiler_params=pltpu.CompilerParams(vmem_limit_bytes=4 * MIB),
    )(voltages)


def frame_spec():
    return pl.BlockSpec((2, GROUP // STEPS, HALF, CHANNELS), lambda i: (0, i, 0, 0))


def whole_spec(shape):
    return pl.BlockSpec(shape, lambda i: (0,) * len(shape))


def front(body, operands, out_shapes, out_specs=None, own_scratch=()):
    if out_specs is None:
        out_specs = [whole_spec(s.shape) for s in out_shapes]
    return pl.pallas_call(
        body,
        grid=(STEPS,),
        in_specs=[frame_spec(), frame_spec()] + [whole_spec(a.shape) for a in operands[2:]],
        out_specs=out_specs,
        out_shape=out_shapes,
        scratch_shapes=[
            *own_scratch,
            pltpu.VMEM((GROUP // STEPS, RADIX, 2, 2 * HALF, LANES), F32),
            pltpu.VMEM((GROUP // STEPS, 2, RADIX, 2, 8, LANES), F32),
            pltpu.VMEM((GROUP * 256, 256), F32),
            pltpu.VMEM((GROUP * 256, 256), F32),
            pltpu.VMEM((GROUP * 256, 256), BF16),
        ],
        compiler_params=pltpu.CompilerParams(vmem_limit_bytes=24 * MIB),
        cost_estimate=pl.CostEstimate(
            flops=700000000, bytes_accessed=3 * MIB, transcendentals=0
        ),
    )(*operands)


def gram_rows(parts_ref, side, out_ref):
    wanted = jnp.bitwise_xor(lax.axis_index("c"), side)
    depth = CHIPS * 2 * LANES
    rows = [
        parts_ref[pl.ds(pl.multiple_of(block * 128 + wanted * 64, 64), 64), :]
        for block in range(CHIPS)
    ]
    same = jnp.concatenate(rows, axis=0)
    cross = jnp.concatenate([same[:, depth:], -same[:, :depth]], axis=1)
    both = jnp.concatenate([same, cross], axis=0)
    result = lax.dot_general(
        both, parts_ref[...], (((1,), (1,)), ((), ())), preferred_element_type=F32
    ) * (1.0 / 4096.0)
    for block in range(CHIPS):
        for part in range(2):
            begin = part * 256 + block * 64
            out_ref[block, part] = result[begin : begin + 64]


def gram_kernel(side, spectra_ref, out_ref, parts_ref):
    depth = CHIPS * 2 * LANES
    for l in range(CHIPS):
        for half in range(2):
            slab = spectra_ref[:, l, half].astype(F32).reshape(STATIONS, 2, 8, LANES)
            for c in range(2):
                begin = c * depth + (l * 2 + half) * LANES
                parts_ref[:, begin : begin + LANES] = (
                    slab[:, c].reshape(STATIONS * 8, LANES).astype(BF16)
                )
    gram_rows(parts_ref, side, out_ref)


def gram(side, spectra):
    return pl.pallas_call(
        functools.partial(gram_kernel, side),
        in_specs=[pl.BlockSpec(memory_space=pltpu.VMEM)],
        out_specs=pl.BlockSpec(memory_space=pltpu.VMEM),
        out_shape=jax.ShapeDtypeStruct((CHIPS, 2, 64, 512), F32),
        scratch_shapes=[pltpu.VMEM((512, 2 * CHIPS * 2 * LANES), BF16)],
        compiler_params=pltpu.CompilerParams(vmem_limit_bytes=16 * MIB),
        cost_estimate=pl.CostEstimate(
            flops=1100000000, bytes_accessed=4 * MIB, transcendentals=0
        ),
    )(spectra)


def own_mask(chip, core):
    row = lax.broadcasted_iota(jnp.int32, (64, 512), 0)
    column = lax.broadcasted_iota(jnp.int32, (64, 512), 1)
    return column == 128 * chip + 64 * core + row


def chip_rows(block, keep_ref, received_ref, own, factor, exponent, out_ref):
    out_ref[0] = (keep_ref[block, 0] + received_ref[block, 0]) * factor
    imaginary = (keep_ref[block, 1] + received_ref[block, 1]) * factor
    out_ref[1] = jnp.where(own, exponent, imaginary)


def far_kernel(
    keep_ref, received_ref, far_ref, farthest_ref, exponent_ref
):
    largest = None
    for block in range(CHIPS):
        for part in range(2):
            total = keep_ref[block, part] + received_ref[block, part]
            here = jnp.max(jnp.abs(total), axis=0, keepdims=True)
            largest = here if largest is None else jnp.maximum(largest, here)
    largest = jnp.maximum(jnp.max(largest, axis=1, keepdims=True), 1e-30)
    exponents = jnp.ceil(jnp.log2(jnp.broadcast_to(largest, (8, LANES))))
    exponent_ref[...] = exponents
    factor, exponent = jnp.exp2(13.0 - exponents)[0:1, 0:1], exponents[0:1, 0:1]
    for step, out_ref in ((2, far_ref), (3, farthest_ref)):
        block = jnp.bitwise_xor(lax.axis_index("l"), step)
        own = own_mask(block, lax.axis_index("c"))
        chip_rows(block, keep_ref, received_ref, own, factor, exponent, out_ref)


def near_kernel(keep_ref, received_ref, exponent_ref, own_ref, near_ref):
    chip = lax.axis_index("l")
    exponents = exponent_ref[...]
    factor, exponent = jnp.exp2(13.0 - exponents)[0:1, 0:1], exponents[0:1, 0:1]
    for part in range(2):
        own_ref[part] = keep_ref[chip, part] + received_ref[chip, part]
    block = jnp.bitwise_xor(chip, 1)
    own = own_mask(block, lax.axis_index("c"))
    chip_rows(block, keep_ref, received_ref, own, factor, exponent, near_ref)


def small(body, operands, out_shapes):
    vmem = pl.BlockSpec(memory_space=pltpu.VMEM)
    return pl.pallas_call(
        body,
        in_specs=[vmem] * len(operands),
        out_specs=[vmem] * len(out_shapes),
        out_shape=[jax.ShapeDtypeStruct(shape, F32) for shape in out_shapes],
        compiler_params=pltpu.CompilerParams(vmem_limit_bytes=8 * MIB),
        cost_estimate=pl.CostEstimate(flops=2000000, bytes_accessed=2 * MIB, transcendentals=0),
    )(*operands)


def widened(ref, diagonal):
    real, imaginary = ref[0], ref[1]
    top = jnp.where(diagonal[0:8], imaginary[0:8], 0.0)
    exponent = jnp.sum(top, axis=1, keepdims=True)[0:1]
    factor = 1.0 / jnp.exp2(13.0 - jnp.broadcast_to(exponent, (8, LANES)))[0:1, 0:1]
    return real * factor, jnp.where(diagonal, 0.0, imaginary) * factor


def other_kernel(far_ref, farthest_ref, out_ref):
    diagonal = own_mask(lax.axis_index("l"), lax.axis_index("c"))
    far, farthest = widened(far_ref, diagonal), widened(farthest_ref, diagonal)
    for part in range(2):
        out_ref[part] = far[part] + farthest[part]


def merge_kernel(own_ref, near_ref, other_ref, out_ref):
    near = widened(near_ref, own_mask(lax.axis_index("l"), lax.axis_index("c")))
    mine = jnp.right_shift(lax.axis_index("l"), 1)
    for part in range(2):
        out_ref[mine, part] = own_ref[part] + near[part]
        out_ref[1 - mine, part] = other_ref[part]


def span_sum(keep, received):
    rows = keep.shape[1:]

    def exchange(values, step):
        route = [(l, l ^ step) for l in range(CHIPS)]
        return lax.ppermute(values.astype(jnp.float16), "l", route).astype(F32)

    far, farthest, exponent = small(
        far_kernel, [keep, received], [rows, rows, (8, LANES)]
    )
    farthest, far = exchange(farthest, 3), exchange(far, 2)
    own, near = small(near_kernel, [keep, received, exponent], [rows, rows])
    (other,) = small(other_kernel, [far, farthest], [rows])
    (both,) = small(merge_kernel, [own, exchange(near, 1), other], [(2,) + rows])
    return jnp.transpose(both, (2, 0, 1, 3))


def on_device(voltages, gains):
    vectors = jnp.asarray(vector_table())
    matrices = jnp.asarray(matrix_table())
    late_lower, late_upper, early_lower, early_upper = (
        jnp.transpose(piece, (2, 0, 1, 3)) for piece in load(voltages)
    )
    forward = [(t, t + 1) for t in range(2 * CHIPS - 1)]
    history_lower = lax.ppermute(late_lower, ("l", "c"), forward)
    history_upper = lax.ppermute(late_upper, ("l", "c"), forward)
    turned_shape = jax.ShapeDtypeStruct((GROUP, 256, 256), BF16)
    turned_scratch = pltpu.VMEM((GROUP, 256, 256), BF16)
    mixed_shape = jax.ShapeDtypeStruct((LANES, 2, 16, LANES), BF16)
    lower, arranged = front(
        late_lower_kernel,
        [early_lower, late_lower, gains, vectors, matrices],
        [turned_shape, jax.ShapeDtypeStruct((RADIX, 2 * INPUTS_DEV, LANES), F32)],
    )
    (mixed,) = front(
        late_upper_kernel,
        [early_upper, late_upper, arranged, vectors, matrices, lower],
        [mixed_shape],
        own_scratch=[turned_scratch],
    )
    (lower,) = front(
        early_lower_kernel,
        [history_lower, early_lower, arranged, vectors, matrices],
        [turned_shape],
    )
    (ready,) = front(
        early_upper_kernel,
        [history_upper, early_upper, arranged, vectors, matrices, lower, mixed],
        [jax.ShapeDtypeStruct((LANES, 2, 2, 16, LANES), BF16)],
        out_specs=[pl.BlockSpec(memory_space=pl.ANY)],
        own_scratch=[
            turned_scratch,
            pltpu.VMEM((LANES, 2, 16, LANES), BF16),
            pltpu.SemaphoreType.DMA((2,)),
        ],
    )
    chunks = ready.reshape(4 * STATIONS, 2, 16, LANES)
    arrived = lax.all_to_all(chunks, ("z", "h", "x", "l"), 0, 0, tiled=True)
    spectra = arrived.reshape(STATIONS, CHIPS, 2, 16, LANES)
    received = lax.ppermute(gram(1, spectra), "c", [(0, 1), (1, 0)])
    return span_sum(gram(0, spectra), received)


def solution(mesh):
    fine = Mesh(mesh.devices.reshape(8, 2, 4, CHIPS, 2), ("z", "h", "x", "l", "c"))
    station, time = ("z", "h", "x"), ("l", "c")
    return jax.shard_map(
        on_device,
        mesh=fine,
        in_specs=(P(station, time, None, None), P(None, station, None)),
        out_specs=P(time, station, None, None),
        check_vma=False,
    )
```

```python
import functools

import jax
import jax.numpy as jnp
import ml_dtypes
import numpy as np
from jax import lax
from jax.experimental import pallas as pl
from jax.experimental.pallas import tpu as pltpu
from jax.sharding import Mesh, PartitionSpec as P

CHANNELS = 2048
TAPS = 16
AVG = 16
RADIX = 16
LANES = 128
HALF = 16
INPUTS_DEV = 8
GROUP = 4
STEPS = 1
STATIONS = 64
CHIPS = 4
MIB = 1024 * 1024
BF16 = jnp.bfloat16
F32 = jnp.float32


def vector_table():
    position = np.arange(TAPS * CHANNELS, dtype=np.float64) + 0.5
    shape_part = np.sinc((position - TAPS * CHANNELS / 2) / CHANNELS)
    taper = np.sin(np.pi * position / (TAPS * CHANNELS)) ** 2
    window = (shape_part * taper).reshape(TAPS, CHANNELS)
    k1 = np.arange(RADIX)[:, None]
    n2 = np.arange(LANES)[None, :]
    angle = 2.0 * np.pi * ((k1 * n2) % CHANNELS) / CHANNELS
    return np.concatenate([window, np.cos(angle), -np.sin(angle)], axis=1).astype(np.float32)


def matrix_table():
    n2 = np.arange(LANES)[:, None]
    k2 = np.arange(LANES)[None, :]
    angle = 2.0 * np.pi * ((n2 * k2) % LANES) / LANES
    cosine, sine = np.cos(angle), np.sin(angle)
    full = np.block([[cosine, -sine], [sine, cosine]]) * CHANNELS**-0.5
    full = full.astype(np.float32)
    high = full.astype(ml_dtypes.bfloat16)
    low = (full - high.astype(np.float32)).astype(ml_dtypes.bfloat16)
    mix = np.zeros((256, 256), np.float32)
    comb = np.zeros((256, 256), np.float32)
    for i in range(INPUTS_DEV):
        for c in range(2):
            for k2 in range(16):
                row = (2 * k2 + c) * INPUTS_DEV + i
                mix[row, (i // GROUP) * 128 + c * 64 + (i % GROUP) * 16 + k2] = 1.0
    for k1 in range(RADIX):
        for j in range(8):
            comb[j * RADIX + k1, k1 * 8 + j] = 1.0
    orders = np.stack([mix, comb]).astype(ml_dtypes.bfloat16)
    return np.concatenate([np.stack([high, low]), orders])


def radix4(values):
    (ar, ai), (br, bi), (cr, ci), (dr, di) = values
    pr, pi, mr, mi = ar + cr, ai + ci, ar - cr, ai - ci
    qr, qi, nr, ni = br + dr, bi + di, br - dr, bi - di
    return [(pr + qr, pi + qi), (mr + ni, mi - nr), (pr - qr, pi - qi), (mr - ni, mi + nr)]


def radix16(values):
    table = [[None] * 4 for _ in range(4)]
    for b in range(4):
        for c, (re, im) in enumerate(radix4([values[4 * a + b] for a in range(4)])):
            turn = b * c
            if turn == 0:
                table[b][c] = (re, im)
            elif turn == 4:
                table[b][c] = (im, -re)
            elif turn == 2:
                root = np.float32(np.sqrt(0.5))
                table[b][c] = ((re + im) * root, (im - re) * root)
            elif turn == 6:
                root = np.float32(np.sqrt(0.5))
                table[b][c] = ((im - re) * root, -(re + im) * root)
            else:
                cosine = np.float32(np.cos(2.0 * np.pi * turn / 16))
                sine = np.float32(np.sin(2.0 * np.pi * turn / 16))
                table[b][c] = (re * cosine + im * sine, im * cosine - re * sine)
    result = [None] * 16
    for c in range(4):
        for d, pair in enumerate(radix4([table[b][c] for b in range(4)])):
            result[c + 4 * d] = pair
    return result


def arrange_gains(gain_ref, matrix_ref, arranged_ref):
    comb = matrix_ref[3, 0:LANES, 0:LANES]
    dot = functools.partial(jnp.dot, preferred_element_type=F32)
    both = gain_ref[...].reshape(2 * INPUTS_DEV, CHANNELS)
    high = both.astype(BF16)
    rest = both - high.astype(F32)
    middle = rest.astype(BF16)
    low = (rest - middle.astype(F32)).astype(BF16)
    pieces = []
    for tile in range(RADIX):
        lanes = slice(tile * LANES, (tile + 1) * LANES)
        pieces.append(
            dot(low[:, lanes], comb) + dot(middle[:, lanes], comb) + dot(high[:, lanes], comb)
        )
    group = lax.broadcasted_iota(jnp.int32, (2 * INPUTS_DEV, LANES), 1) // 8
    for bit in (1, 2, 4, 8):
        clear = jnp.bitwise_and(group, bit) == 0
        for tile in range(RADIX):
            if tile & bit == 0:
                a, b = pieces[tile], pieces[tile | bit]
                pieces[tile] = jnp.where(clear, a, pltpu.roll(b, 8 * bit, 1))
                pieces[tile | bit] = jnp.where(clear, pltpu.roll(a, LANES - 8 * bit, 1), b)
    for k1 in range(RADIX):
        arranged_ref[k1] = pieces[k1]


def analyse(hist_ref, cur_ref, j, vector_ref, stage, scratch):
    ext, filtered = scratch
    for n1 in range(RADIX):
        lanes = slice(n1 * LANES, (n1 + 1) * LANES)
        for c in range(2):
            ext[n1, c, 0:HALF, :] = hist_ref[c, j, :, lanes].astype(F32)
            ext[n1, c, HALF : 2 * HALF, :] = cur_ref[c, j, :, lanes].astype(F32)
    for n1 in range(RADIX):
        lanes = slice(n1 * LANES, (n1 + 1) * LANES)
        sums = [None] * 4
        for t in range(TAPS):
            weight = vector_ref[t : t + 1, lanes]
            for c in range(2):
                for block in range(2):
                    begin = block * 8 + 1 + t
                    term = ext[n1, c, begin : begin + 8, :] * weight
                    slot = 2 * c + block
                    sums[slot] = term if t == 0 else sums[slot] + term
        for c in range(2):
            for block in range(2):
                filtered[block, n1, c] = sums[2 * c + block]
    for block in range(2):
        values = [(filtered[block, n1, 0], filtered[block, n1, 1]) for n1 in range(RADIX)]
        for k1, (re, im) in enumerate(radix16(values)):
            cosine = vector_ref[k1 : k1 + 1, CHANNELS : CHANNELS + LANES]
            sine = vector_ref[k1 : k1 + 1, CHANNELS + LANES : CHANNELS + 2 * LANES]
            rows = slice(k1 * HALF + block * 8, k1 * HALF + block * 8 + 8)
            stage[rows, 0:LANES] = re * cosine - im * sine
            stage[rows, LANES : 2 * LANES] = re * sine + im * cosine


def finish(gain_ref, matrix_ref, turned, first, stage, result, equal):
    dot = functools.partial(jnp.dot, preferred_element_type=F32)
    whole = stage[...]
    high = whole.astype(BF16)
    low = (whole - high.astype(F32)).astype(BF16)
    result[...] = dot(high, matrix_ref[0]) + dot(high, matrix_ref[1]) + dot(low, matrix_ref[0])
    for i in range(GROUP):
        for k1 in range(RADIX):
            rows = slice(i * 256 + k1 * HALF, i * 256 + (k1 + 1) * HALF)
            re, im = result[rows, 0:LANES], result[rows, LANES : 2 * LANES]
            place = first + i
            gain_re = gain_ref[k1, place : place + 1, :]
            gain_im = gain_ref[k1, INPUTS_DEV + place : INPUTS_DEV + place + 1, :]
            equal[rows, 0:LANES] = (re * gain_re - im * gain_im).astype(BF16)
            equal[rows, LANES : 2 * LANES] = (re * gain_im + im * gain_re).astype(BF16)
    across = jnp.transpose(equal[...].astype(F32)).astype(BF16)
    for i in range(GROUP):
        turned[i] = across[:, i * 256 : (i + 1) * 256]


def filter_transform(hist_ref, cur_ref, gain_ref, vector_ref, matrix_ref, first, turned, scratch):
    ext, filtered, stage, result, equal = scratch
    step = pl.program_id(0)

    for j in range(GROUP // STEPS):
        rows = pl.ds(pl.multiple_of((step * (GROUP // STEPS) + j) * 256, 256), 256)
        analyse(
            hist_ref, cur_ref, j, vector_ref, stage.at[rows], (ext.at[j], filtered.at[j])
        )

    @pl.when(step == STEPS - 1)
    def _():
        finish(gain_ref, matrix_ref, turned, first, stage, result, equal)


def mix(matrix_ref, lower, upper, group):
    slabs = [
        half[:, c * LANES + group * 16 : c * LANES + (group + 1) * 16, :].reshape(64, 256)
        for half in (lower, upper)
        for c in range(2)
    ]
    piece = jnp.concatenate(slabs, axis=0)
    return jnp.dot(matrix_ref[2], piece, preferred_element_type=F32).astype(BF16)


def mix_all(matrix_ref, lower, upper, out_ref):
    for group in range(8):
        rows = slice(group * 16, (group + 1) * 16)
        mixed = mix(matrix_ref, lower, upper, group)
        for h in range(2):
            out_ref[rows, h] = mixed[:, h * LANES : (h + 1) * LANES].reshape(16, 16, LANES)


def late_lower_kernel(
    hist_ref, cur_ref, gain_ref, vector_ref, matrix_ref, turned, arranged_ref, *scratch
):
    @pl.when(pl.program_id(0) == 0)
    def _():
        arrange_gains(gain_ref, matrix_ref, arranged_ref)

    filter_transform(
        hist_ref, cur_ref, arranged_ref, vector_ref, matrix_ref, 0, turned, scratch
    )


def late_upper_kernel(
    hist_ref, cur_ref, gain_ref, vector_ref, matrix_ref, lower_ref, mixed_ref, turned, *scratch
):
    filter_transform(
        hist_ref, cur_ref, gain_ref, vector_ref, matrix_ref, GROUP, turned, scratch
    )

    @pl.when(pl.program_id(0) == STEPS - 1)
    def _():
        mix_all(matrix_ref, lower_ref, turned, mixed_ref)


def early_lower_kernel(hist_ref, cur_ref, gain_ref, vector_ref, matrix_ref, turned, *scratch):
    filter_transform(hist_ref, cur_ref, gain_ref, vector_ref, matrix_ref, 0, turned, scratch)


def early_upper_kernel(
    hist_ref,
    cur_ref,
    gain_ref,
    vector_ref,
    matrix_ref,
    lower_ref,
    mixed_ref,
    out_ref,
    turned,
    early_ref,
    sems,
    *scratch,
):
    step = pl.program_id(0)
    late_copy = pltpu.make_async_copy(mixed_ref, out_ref.at[:, :, 1], sems.at[0])
    early_copy = pltpu.make_async_copy(early_ref, out_ref.at[:, :, 0], sems.at[1])

    @pl.when(step == 0)
    def _():
        late_copy.start()

    filter_transform(
        hist_ref, cur_ref, gain_ref, vector_ref, matrix_ref, GROUP, turned, scratch
    )

    @pl.when(step == STEPS - 1)
    def _():
        mix_all(matrix_ref, lower_ref, turned, early_ref)
        early_copy.start()
        early_copy.wait()
        late_copy.wait()


def load_kernel(voltages_ref, *refs):
    outs, sems = refs[:4], refs[4]
    copies = []
    for n, out in enumerate(outs):
        source = voltages_ref.at[pl.ds((n % 2) * GROUP, GROUP), pl.ds((1 - n // 2) * HALF, HALF)]
        copies.append(pltpu.make_async_copy(source, out, sems.at[n]))
    for copy in copies:
        copy.start()
    for copy in copies:
        copy.wait()


def load(voltages):
    shape = jax.ShapeDtypeStruct((GROUP, HALF, 2, CHANNELS), BF16)
    return pl.pallas_call(
        load_kernel,
        in_specs=[pl.BlockSpec(memory_space=pltpu.HBM)],
        out_specs=[pl.BlockSpec(memory_space=pltpu.VMEM)] * 4,
        out_shape=[shape] * 4,
        scratch_shapes=[pltpu.SemaphoreType.DMA((4,))],
        compiler_params=pltpu.CompilerParams(vmem_limit_bytes=56 * MIB),
    )(voltages)


def frame_spec():
    return pl.BlockSpec((2, GROUP // STEPS, HALF, CHANNELS), lambda i: (0, i, 0, 0))


def whole_spec(shape):
    return pl.BlockSpec(shape, lambda i: (0,) * len(shape))


def front(body, operands, out_shapes, out_specs=None, own_scratch=()):
    if out_specs is None:
        out_specs = [whole_spec(s.shape) for s in out_shapes]
    return pl.pallas_call(
        body,
        grid=(STEPS,),
        in_specs=[frame_spec(), frame_spec()] + [whole_spec(a.shape) for a in operands[2:]],
        out_specs=out_specs,
        out_shape=out_shapes,
        scratch_shapes=[
            *own_scratch,
            pltpu.VMEM((GROUP // STEPS, RADIX, 2, 2 * HALF, LANES), F32),
            pltpu.VMEM((GROUP // STEPS, 2, RADIX, 2, 8, LANES), F32),
            pltpu.VMEM((GROUP * 256, 256), F32),
            pltpu.VMEM((GROUP * 256, 256), F32),
            pltpu.VMEM((GROUP * 256, 256), BF16),
        ],
        compiler_params=pltpu.CompilerParams(vmem_limit_bytes=24 * MIB),
        cost_estimate=pl.CostEstimate(
            flops=700000000, bytes_accessed=3 * MIB, transcendentals=0
        ),
    )(*operands)


def gram_rows(parts_ref, side, out_ref):
    wanted = jnp.bitwise_xor(lax.axis_index("c"), side)
    depth = CHIPS * 2 * LANES
    rows = [
        parts_ref[pl.ds(pl.multiple_of(block * 128 + wanted * 64, 64), 64), :]
        for block in range(CHIPS)
    ]
    same = jnp.concatenate(rows, axis=0)
    cross = jnp.concatenate([same[:, depth:], -same[:, :depth]], axis=1)
    both = jnp.concatenate([same, cross], axis=0)
    result = lax.dot_general(
        both, parts_ref[...], (((1,), (1,)), ((), ())), preferred_element_type=F32
    ) * (1.0 / 4096.0)
    for block in range(CHIPS):
        for part in range(2):
            begin = part * 256 + block * 64
            out_ref[block, part] = result[begin : begin + 64]


def gram_kernel(side, spectra_ref, out_ref, parts_ref):
    depth = CHIPS * 2 * LANES
    for l in range(CHIPS):
        for half in range(2):
            slab = spectra_ref[:, l, half].astype(F32).reshape(STATIONS, 2, 8, LANES)
            for c in range(2):
                begin = c * depth + (l * 2 + half) * LANES
                parts_ref[:, begin : begin + LANES] = (
                    slab[:, c].reshape(STATIONS * 8, LANES).astype(BF16)
                )
    gram_rows(parts_ref, side, out_ref)


def gram(side, spectra):
    return pl.pallas_call(
        functools.partial(gram_kernel, side),
        in_specs=[pl.BlockSpec(memory_space=pltpu.VMEM)],
        out_specs=pl.BlockSpec(memory_space=pltpu.VMEM),
        out_shape=jax.ShapeDtypeStruct((CHIPS, 2, 64, 512), F32),
        scratch_shapes=[pltpu.VMEM((512, 2 * CHIPS * 2 * LANES), BF16)],
        compiler_params=pltpu.CompilerParams(vmem_limit_bytes=16 * MIB),
        cost_estimate=pl.CostEstimate(
            flops=1100000000, bytes_accessed=4 * MIB, transcendentals=0
        ),
    )(spectra)


def own_mask(chip, core):
    row = lax.broadcasted_iota(jnp.int32, (64, 512), 0)
    column = lax.broadcasted_iota(jnp.int32, (64, 512), 1)
    return column == 128 * chip + 64 * core + row


def chip_rows(block, keep_ref, received_ref, own, factor, exponent, out_ref):
    out_ref[0] = (keep_ref[block, 0] + received_ref[block, 0]) * factor
    imaginary = (keep_ref[block, 1] + received_ref[block, 1]) * factor
    out_ref[1] = jnp.where(own, exponent, imaginary)


def far_kernel(
    keep_ref, received_ref, far_ref, farthest_ref, exponent_ref
):
    largest = None
    for block in range(CHIPS):
        for part in range(2):
            total = keep_ref[block, part] + received_ref[block, part]
            here = jnp.max(jnp.abs(total), axis=0, keepdims=True)
            largest = here if largest is None else jnp.maximum(largest, here)
    largest = jnp.maximum(jnp.max(largest, axis=1, keepdims=True), 1e-30)
    exponents = jnp.ceil(jnp.log2(jnp.broadcast_to(largest, (8, LANES))))
    exponent_ref[...] = exponents
    factor, exponent = jnp.exp2(13.0 - exponents)[0:1, 0:1], exponents[0:1, 0:1]
    for step, out_ref in ((2, far_ref), (3, farthest_ref)):
        block = jnp.bitwise_xor(lax.axis_index("l"), step)
        own = own_mask(block, lax.axis_index("c"))
        chip_rows(block, keep_ref, received_ref, own, factor, exponent, out_ref)


def near_kernel(keep_ref, received_ref, exponent_ref, own_ref, near_ref):
    chip = lax.axis_index("l")
    exponents = exponent_ref[...]
    factor, exponent = jnp.exp2(13.0 - exponents)[0:1, 0:1], exponents[0:1, 0:1]
    for part in range(2):
        own_ref[part] = keep_ref[chip, part] + received_ref[chip, part]
    block = jnp.bitwise_xor(chip, 1)
    own = own_mask(block, lax.axis_index("c"))
    chip_rows(block, keep_ref, received_ref, own, factor, exponent, near_ref)


def small(body, operands, out_shapes):
    vmem = pl.BlockSpec(memory_space=pltpu.VMEM)
    return pl.pallas_call(
        body,
        in_specs=[vmem] * len(operands),
        out_specs=[vmem] * len(out_shapes),
        out_shape=[jax.ShapeDtypeStruct(shape, F32) for shape in out_shapes],
        compiler_params=pltpu.CompilerParams(vmem_limit_bytes=8 * MIB),
        cost_estimate=pl.CostEstimate(flops=2000000, bytes_accessed=2 * MIB, transcendentals=0),
    )(*operands)


def widened(ref, diagonal):
    real, imaginary = ref[0], ref[1]
    top = jnp.where(diagonal[0:8], imaginary[0:8], 0.0)
    exponent = jnp.sum(top, axis=1, keepdims=True)[0:1]
    factor = 1.0 / jnp.exp2(13.0 - jnp.broadcast_to(exponent, (8, LANES)))[0:1, 0:1]
    return real * factor, jnp.where(diagonal, 0.0, imaginary) * factor


def other_kernel(far_ref, farthest_ref, out_ref):
    diagonal = own_mask(lax.axis_index("l"), lax.axis_index("c"))
    far, farthest = widened(far_ref, diagonal), widened(farthest_ref, diagonal)
    for part in range(2):
        out_ref[part] = far[part] + farthest[part]


def merge_kernel(own_ref, near_ref, other_ref, out_ref):
    near = widened(near_ref, own_mask(lax.axis_index("l"), lax.axis_index("c")))
    mine = jnp.right_shift(lax.axis_index("l"), 1)
    for part in range(2):
        out_ref[mine, part] = own_ref[part] + near[part]
        out_ref[1 - mine, part] = other_ref[part]


def span_sum(keep, received):
    rows = keep.shape[1:]

    def exchange(values, step):
        route = [(l, l ^ step) for l in range(CHIPS)]
        return lax.ppermute(values.astype(jnp.float16), "l", route).astype(F32)

    far, farthest, exponent = small(
        far_kernel, [keep, received], [rows, rows, (8, LANES)]
    )
    farthest, far = exchange(farthest, 3), exchange(far, 2)
    own, near = small(near_kernel, [keep, received, exponent], [rows, rows])
    (other,) = small(other_kernel, [far, farthest], [rows])
    (both,) = small(merge_kernel, [own, exchange(near, 1), other], [(2,) + rows])
    return jnp.transpose(both, (2, 0, 1, 3))


def on_device(voltages, gains):
    vectors = jnp.asarray(vector_table())
    matrices = jnp.asarray(matrix_table())
    late_lower, late_upper, early_lower, early_upper = (
        jnp.transpose(piece, (2, 0, 1, 3)) for piece in load(voltages)
    )
    forward = [(t, t + 1) for t in range(2 * CHIPS - 1)]
    history_lower = lax.ppermute(late_lower, ("l", "c"), forward)
    history_upper = lax.ppermute(late_upper, ("l", "c"), forward)
    turned_shape = jax.ShapeDtypeStruct((GROUP, 256, 256), BF16)
    turned_scratch = pltpu.VMEM((GROUP, 256, 256), BF16)
    mixed_shape = jax.ShapeDtypeStruct((LANES, 2, 16, LANES), BF16)
    lower, arranged = front(
        late_lower_kernel,
        [early_lower, late_lower, gains, vectors, matrices],
        [turned_shape, jax.ShapeDtypeStruct((RADIX, 2 * INPUTS_DEV, LANES), F32)],
    )
    (mixed,) = front(
        late_upper_kernel,
        [early_upper, late_upper, arranged, vectors, matrices, lower],
        [mixed_shape],
        own_scratch=[turned_scratch],
    )
    (lower,) = front(
        early_lower_kernel,
        [history_lower, early_lower, arranged, vectors, matrices],
        [turned_shape],
    )
    (ready,) = front(
        early_upper_kernel,
        [history_upper, early_upper, arranged, vectors, matrices, lower, mixed],
        [jax.ShapeDtypeStruct((LANES, 2, 2, 16, LANES), BF16)],
        out_specs=[pl.BlockSpec(memory_space=pl.ANY)],
        own_scratch=[
            turned_scratch,
            pltpu.VMEM((LANES, 2, 16, LANES), BF16),
            pltpu.SemaphoreType.DMA((2,)),
        ],
    )
    chunks = ready.reshape(4 * STATIONS, 2, 16, LANES)
    arrived = lax.all_to_all(chunks, ("z", "h", "x", "l"), 0, 0, tiled=True)
    spectra = arrived.reshape(STATIONS, CHIPS, 2, 16, LANES)
    received = lax.ppermute(gram(1, spectra), "c", [(0, 1), (1, 0)])
    return span_sum(gram(0, spectra), received)


def solution(mesh):
    fine = Mesh(mesh.devices.reshape(8, 2, 4, CHIPS, 2), ("z", "h", "x", "l", "c"))
    station, time = ("z", "h", "x"), ("l", "c")
    return jax.shard_map(
        on_device,
        mesh=fine,
        in_specs=(P(station, time, None, None), P(None, station, None)),
        out_specs=P(time, station, None, None),
        check_vma=False,
    )
```
